256 devices in a mesh: gx: 8 (over y, z_hi), gy: 8 (over x, core), gz: 4 (over z_lo).
Axes of the slice: x: 4, y: 4, z: 8 (z_hi: 2, z_lo: 4; z = z_hi * 4 + z_lo), core: 2. Of those that a mesh axis runs over, the one named last changes fastest.
Arguments:
- tokens: bfloat16 [1024, 4096], P(('gy', 'gx'), 'gz'), may hold values from -6 to 6
- gate_weight: bfloat16 [4096, 14784], P(('gz', 'gy'), 'gx'), may hold values from -0.09375 to 0.09375
- up_weight: bfloat16 [4096, 14784], P(('gz', 'gy'), 'gx'), may hold values from -0.09375 to 0.09375
- down_weight: bfloat16 [14784, 4096], P(('gx', 'gy'), 'gz'), may hold values from -0.046875 to 0.046875
- cotangent: bfloat16 [1024, 4096], P(('gy', 'gx'), 'gz'), may hold values from -6 to 6
Outputs:
- mixed: bfloat16 [1024, 4096], P(('gy', 'gx'), 'gz')
- grad_tokens: bfloat16 [1024, 4096], P(('gy', 'gx'), 'gz')
- grad_gate: float32 [4096, 14784], P(('gz', 'gy'), 'gx')
- grad_up: float32 [4096, 14784], P(('gz', 'gy'), 'gx')
- grad_down: float32 [14784, 4096], P(('gx', 'gy'), 'gz')
The draws below stay inside these ranges and needn't reach their ends.
All inputs are finite; a program needn't handle non-finite values.
Results may differ from the reference program's by a relative error of at most 0.005.
Values may be sent and summed in bfloat16 or wider, within the bound.
A program may use at most 128 MiB of HBM per device.

```python
import math
import jax
import jax.numpy as jnp
from jax import lax

D = 4096
FF = 14784
TOKENS = 1024


def steps_of(rng, extent, pieces, low, high):
    level, own = 1.0, jax.random.fold_in(rng, 6)
    for dim, blocks in pieces:
        heights = jnp.exp(jax.random.uniform(jax.random.fold_in(own, dim), (blocks,), jnp.float32, low / len(pieces), high / len(pieces)))
        level = level * jnp.repeat(heights, extent[dim] // blocks).reshape([-1 if axis == dim else 1 for axis in range(len(extent))])
    return level


def gaussian(own_key, dims, deviation, reach, pieces=(), dtype=jnp.bfloat16):
    loudness = steps_of(own_key, dims, pieces, -0.22, 0.18) if pieces else 1.0
    entries = jax.random.normal(own_key, dims, jnp.float32) * deviation * loudness
    return jnp.minimum(jnp.maximum(entries, -reach), reach).astype(dtype)


def setup_inputs(seed: int = 0) -> dict:
    key_list = jax.random.split(jax.random.key(seed), 6)
    return {
        "tokens": gaussian(key_list[0], (TOKENS, D), 1.0, 6.0, ((0, 64), (1, 4))),
        "gate_weight": gaussian(key_list[1], (D, FF), D ** -0.5, 0.09375, ((0, 32), (1, 8))),
        "up_weight": gaussian(key_list[2], (D, FF), D ** -0.5, 0.09375, ((0, 32), (1, 8))),
        "down_weight": gaussian(key_list[3], (FF, D), FF ** -0.5, 0.046875, ((0, 64), (1, 4))),
        "cotangent": gaussian(key_list[4], (TOKENS, D), 1.0, 6.0, ((0, 64), (1, 4))),
    }


def contract_last(left, right):
    return lax.dot_general(left, right, (((1,), (1,)), ((), ())), preferred_element_type=jnp.float32)

def contract_first(left, right):
    return lax.dot_general(left, right, (((0,), (0,)), ((), ())), preferred_element_type=jnp.float32)

def reference(tokens, gate_weight, up_weight, down_weight, cotangent):
    gate = jnp.dot(tokens, gate_weight, preferred_element_type=jnp.float32)
    up = jnp.dot(tokens, up_weight, preferred_element_type=jnp.float32)
    sigma = jax.nn.sigmoid(gate)
    swish = gate * sigma
    hidden = (swish * up).astype(jnp.bfloat16)
    mixed = jnp.dot(hidden, down_weight, preferred_element_type=jnp.float32).astype(jnp.bfloat16)
    grad_hidden = contract_last(cotangent, down_weight)
    grad_gate_act = (grad_hidden * up * sigma * (1.0 + gate * (1.0 - sigma))).astype(jnp.bfloat16)
    grad_up_act = (grad_hidden * swish).astype(jnp.bfloat16)
    grad_tokens = (contract_last(grad_gate_act, gate_weight) + contract_last(grad_up_act, up_weight)).astype(jnp.bfloat16)
    factor = 1.0 / math.sqrt(TOKENS)
    grad_gate = contract_first(tokens, grad_gate_act) * factor
    grad_up = contract_first(tokens, grad_up_act) * factor
    grad_down = contract_first(hidden, cotangent) * factor
    return (mixed, grad_tokens, grad_gate, grad_up, grad_down)
```

```python
import functools
import math

import jax
import jax.numpy as jnp
from jax import lax
from jax.experimental import pallas as pl
from jax.experimental.pallas import tpu as pltpu
from jax.sharding import PartitionSpec as P

BF = jnp.bfloat16
F32 = jnp.float32
MESH_ID = pl.DeviceIdType.MESH


def dot_nn(a, b):
    return lax.dot_general(a, b, (((1,), (0,)), ((), ())), preferred_element_type=F32)


def dot_nt(a, b):
    return lax.dot_general(a, b, (((1,), (1,)), ((), ())), preferred_element_type=F32)


LAYOUT = {}
COUNT = 0
for name, size in (
    ("zh", 2), ("y", 6), ("x", 6), ("wx", 4), ("wc", 4), ("wd", 1),
    ("rh", 4), ("rp", 4), ("ag", 12), ("ox", 8), ("oy", 8), ("oz", 2),
    ("gc", 8), ("gx", 8), ("gd", 1),
):
    LAYOUT[name] = COUNT
    COUNT += size


def kernel(
    factor,
    tok_ref, cot_ref, wl_ref, wd_ref,
    mixed_ref, gtok_ref, ggate_ref, gup_ref, gdown_ref,
    acts, w, wd, zs_h, zr_h, own_h, zs_p, zr_p, own_p, mids, tok_t, hid_t,
    o_send, o_recv, o_own, y_own, y_recv, z_send, z_recv,
    gc_send, gc_recv, g_own, gx_send, gx_recv, gd_send, gd_recv,
    send, recv,
):
    gx, gy, z = lax.axis_index("gx"), lax.axis_index("gy"), lax.axis_index("gz")
    y, h = gx // 2, gx % 2
    x, c = gy // 2, gy % 2
    oc = 1 - c

    def at(dx=0, dc=0, dy=0, dh=0, dz=0):
        px, py, pz = (x + dx) % 4, (y + dy) % 4, (z + dz) % 4
        ph, pc = (h + dh) % 2, (c + dc) % 2
        return (py * 2 + ph, px * 2 + pc, pz)

    def copy(src, dst, who, name, s_off, r_off=None):
        r_off = s_off if r_off is None else r_off
        return pltpu.make_async_remote_copy(
            src_ref=src, dst_ref=dst,
            send_sem=send.at[LAYOUT[name] + s_off], recv_sem=recv.at[LAYOUT[name] + r_off],
            device_id=who, device_id_type=MESH_ID,
        )

    started = []

    def go(*args):
        cp = copy(*args)
        cp.start()
        started.append(cp)
        return cp

    peers = (
        [at(dx=k) for k in (1, 2, 3)] + [at(dy=k) for k in (1, 2, 3)]
        + [at(dz=k) for k in (1, 2, 3)] + [at(dh=1), at(dc=1)]
    )
    barrier = pltpu.get_barrier_semaphore()
    for who in peers:
        pl.semaphore_signal(barrier, inc=1, device_id=who, device_id_type=MESH_ID)
    acts[0, 0:16, :] = cot_ref[...]
    acts[1, 0:16, :] = tok_ref[...]
    wd[pl.ds(pl.multiple_of(c * 256, 256), 256), :] = wd_ref[...]
    row_own = pl.multiple_of((x * 2 + c) * 128, 128)
    w[pl.ds(row_own, 128), :] = wl_ref[x]
    pl.semaphore_wait(barrier, len(peers))

    zh = [
        go((cot_ref, tok_ref)[i], acts.at[i, pl.ds(16, 16), :], at(dh=1), "zh", i) for i in (0, 1)
    ]
    wd_slot = wd.at[pl.ds(pl.multiple_of(c * 256, 256), 256), :]
    wdc = go(wd_ref, wd_slot, at(dc=1), "wd", 0)
    wx = {}
    for r in (1, 3, 2):
        wx[r] = go(wl_ref.at[(x + r) % 4], w.at[pl.ds(row_own, 128), :], at(dx=r), "wx", r)
    wc = [go(wl_ref.at[x], w.at[pl.ds(row_own, 128), :], at(dc=1), "wc", 0)]

    def spread_y(i):
        zh[i].wait_recv()
        src = acts.at[i, pl.ds(0, 32), :]
        return [
            go(src, acts.at[i, pl.ds(32 * m, 32), :], at(dy=m), "y", i * 3 + m - 1) for m in (1, 2, 3)
        ]

    def spread_x(i, copies):
        for cp in copies:
            cp.wait_recv()
        src = acts.at[i, pl.ds(0, 128), :]
        return {
            k: go(src, acts.at[i, pl.ds(128 * k, 128), :], at(dx=k), "x", i * 3 + k - 1)
            for k in (1, 3, 2)
        }

    def z_send_block(k, src, dst, name):
        @pl.when(z != k)
        def _():
            r = (k - z + 4) % 4
            copy(src.at[k], dst.at[r], (gx, gy, k), name, k, r).start()

    def hidden_grad(k):
        def tile(j, carry):
            rows = pl.ds(pl.multiple_of(j * 256, 256), 256)
            part = dot_nt(acts[0, 128 * k:128 * (k + 1), :], wd[rows, :])
            zs_h[k, :, rows] = part.astype(BF)

            @pl.when(z == k)
            def _():
                own_h[:, rows] = part

            return carry

        lax.fori_loop(0, 2, tile, 0)
        z_send_block(k, zs_h, zr_h, "rh")

    def gate_up(k):
        def tile(j, carry):
            cols = pl.ds(pl.multiple_of(j * 256, 256), 256)
            part = dot_nn(acts[1, 128 * k:128 * (k + 1), :], w[:, cols])
            zs_p[k, :, cols] = part.astype(BF)

            @pl.when(z == k)
            def _():
                own_p[:, cols] = part

            return carry

        lax.fori_loop(0, 4, tile, 0)
        z_send_block(k, zs_p, zr_p, "rp")

    cot_y = spread_y(0)
    tok_y = spread_y(1)
    cot_x = spread_x(0, cot_y)
    wdc.wait_recv()
    hidden_grad(0)
    for r in (1, 3, 2):
        wx[r].wait_recv()
        rows = pl.ds(pl.multiple_of(((x - r + 4) % 4 * 2 + c) * 128, 128), 128)
        wc.append(go(w.at[rows, :], w.at[rows, :], at(dc=1), "wc", r))
    tok_x = spread_x(1, tok_y)
    for k in (1, 3, 2):
        cot_x[k].wait_recv()
        hidden_grad(k)
    for cp in wc:
        cp.wait_recv()
    gate_up(0)
    for k in (1, 3, 2):
        tok_x[k].wait_recv()
        gate_up(k)

    def flip(k, carry):
        rows = pl.ds(pl.multiple_of(k * 128, 128), 128)
        tok_t[:, rows] = acts[1, rows, :].T
        return carry

    lax.fori_loop(0, 4, flip, 0)

    for r in (1, 2, 3):
        copy(zs_h.at[0], zr_h.at[r], at(dz=r), "rh", 0, r).wait_recv()
        copy(zs_p.at[0], zr_p.at[r], at(dz=r), "rp", 0, r).wait_recv()

    def mix(j, carry):
        cols = pl.ds(pl.multiple_of(j * 128, 128), 128)
        upper = pl.ds(pl.multiple_of(j * 128 + 512, 128), 128)

        def total(own, got, where):
            return (
                (own[:, where] + got[1, :, where].astype(F32))
                + (got[2, :, where].astype(F32) + got[3, :, where].astype(F32))
            )

        gate = total(own_p, zr_p, cols)
        up = total(own_p, zr_p, upper)
        grad = total(own_h, zr_h, cols)
        sigma = jax.nn.sigmoid(gate)
        swish = gate * sigma
        mids[0, z, :, cols] = (grad * swish).astype(BF)
        mids[1, z, :, cols] = (grad * up * sigma * (1.0 + gate * (1.0 - sigma))).astype(BF)
        mids[2, z, :, cols] = (swish * up).astype(BF)
        return carry

    lax.fori_loop(0, 4, mix, 0)
    for m in (0, 1, 2):
        for r in (1, 3, 2):
            go(mids.at[m, z], mids.at[m, z], at(dz=r), "ag", m * 4 + r)

    def arrived(m):
        for r in (1, 2, 3):
            slot = mids.at[m, (z - r + 4) % 4]
            copy(slot, slot, at(dz=r), "ag", m * 4 + r).wait_recv()

    def whole(m):
        return mids[m].reshape(512, 512)

    def weight_grad(m):
        cps = []
        for r in (1, 3, 2, 0):
            to = (x + r) % 4
            rows = pl.ds(pl.multiple_of((to * 2 + oc) * 128, 128), 128)
            gc_send[m, r] = (dot_nn(tok_t[rows, :], whole(m)) * factor).astype(BF)
            cps.append(go(gc_send.at[m, r], gc_recv.at[m, r], at(dc=1), "gc", m * 4 + r))
        for r, cp in zip((1, 3, 2, 0), cps):
            to = (x + r) % 4
            rows = pl.ds(pl.multiple_of((to * 2 + c) * 128, 128), 128)
            mine = dot_nn(tok_t[rows, :], whole(m)) * factor
            cp.wait_recv()
            both = mine + gc_recv[m, r].astype(F32)
            if r:
                gx_send[m, r] = both.astype(BF)
                go(gx_send.at[m, r], gx_recv.at[m, r], at(dx=r), "gx", m * 4 + r)
            else:
                g_own[m] = both

    def out_block(n, k, value):
        def tile(j, carry):
            cols = pl.ds(pl.multiple_of(j * 256, 256), 256)
            part = value(cols)
            if k:
                o_send[n, k, :, cols] = part.astype(BF)
            else:
                o_own[n, :, cols] = part
            return carry

        lax.fori_loop(0, 4, tile, 0)
        if k:
            go(o_send.at[n, k], o_recv.at[n, k], at(dx=4 - k), "ox", n * 4 + k)

    arrived(0)
    weight_grad(0)
    arrived(1)
    for k in (1, 3, 2, 0):
        out_block(
            0, k,
            lambda cols, k=k: dot_nt(mids[1, k], w[cols, 0:512]) + dot_nt(mids[0, k], w[cols, 512:1024]),
        )
    weight_grad(1)
    arrived(2)
    for k in (1, 3, 2, 0):
        out_block(1, k, lambda cols, k=k: dot_nn(mids[2, k], wd[:, cols]))

    for k in range(4):
        hid_t[:, 128 * k:128 * (k + 1)] = mids[2, k].T
    theirs = pl.ds(pl.multiple_of(oc * 256, 256), 256)
    ours = pl.ds(pl.multiple_of(c * 256, 256), 256)

    def down_theirs(j, carry):
        cols = pl.ds(pl.multiple_of(j * 256, 256), 256)
        gd_send[:, cols] = (dot_nn(hid_t[theirs, :], acts[0, :, cols]) * factor).astype(BF)
        return carry

    lax.fori_loop(0, 4, down_theirs, 0)
    gd = go(gd_send, gd_recv, at(dc=1), "gd", 0)

    def down_ours(j, carry):
        cols = pl.ds(pl.multiple_of(j * 256, 256), 256)
        gdown_ref[:, cols] = dot_nn(hid_t[ours, :], acts[0, :, cols]) * factor
        return carry

    lax.fori_loop(0, 4, down_ours, 0)

    oy = {}
    for n in (0, 1):
        for k in (1, 2, 3):
            copy(o_send.at[n, k], o_recv.at[n, k], at(dx=4 - k), "ox", n * 4 + k).wait_recv()
        y_own[n] = (o_own[n] + o_recv[n, 1].astype(F32)) + (
            o_recv[n, 2].astype(F32) + o_recv[n, 3].astype(F32)
        )
        for m in (1, 3, 2):
            oy[n, m] = go(
                y_own.at[n, pl.ds(32 * m, 32), :], y_recv.at[n, m], at(dy=4 - m), "oy", n * 4 + m
            )
    oz = []
    for n in (0, 1):
        for m in (1, 2, 3):
            oy[n, m].wait_recv()
        z_send[n] = (y_own[n, 0:32, :] + y_recv[n, 1]) + (y_recv[n, 2] + y_recv[n, 3])
        oz.append(go(z_send.at[n, pl.ds(16, 16), :], z_recv.at[n], at(dh=1), "oz", n))

    gd.wait_recv()
    gdown_ref[...] += gd_recv[...].astype(F32)
    for m, out in ((0, gup_ref), (1, ggate_ref)):
        for r in (1, 2, 3):
            copy(gx_send.at[m, r], gx_recv.at[m, r], at(dx=r), "gx", m * 4 + r).wait_recv()
            cols = pl.ds(pl.multiple_of((x - r + 4) % 4 * 512, 512), 512)
            out[:, cols] = gx_recv[m, r].astype(F32)
        out[:, pl.ds(pl.multiple_of(x * 512, 512), 512)] = g_own[m]
    for n, out in ((0, gtok_ref), (1, mixed_ref)):
        oz[n].wait_recv()
        out[...] = (z_send[n, 0:16, :] + z_recv[n]).astype(BF)

    for cp in started:
        cp.wait_send()
    for k in range(4):
        @pl.when(z != k)
        def _():
            copy(zs_h.at[k], zr_h.at[1], (gx, gy, k), "rh", k, 1).wait_send()
            copy(zs_p.at[k], zr_p.at[1], (gx, gy, k), "rp", k, 1).wait_send()


def body(tokens, gate_weight, up_weight, down_weight, cotangent):
    unit = gate_weight.shape[1] // 8
    gap = 256 - unit

    def widen(a):
        return jnp.pad(a.reshape(128, 8, unit), ((0, 0), (0, 0), (0, gap))).reshape(128, 4, 512)

    wl = jnp.concatenate([widen(gate_weight), widen(up_weight)], axis=2).transpose(1, 0, 2)
    wd = jnp.pad(down_weight, ((0, gap), (0, 0)))
    vmem = pl.BlockSpec(memory_space=pltpu.VMEM)
    factor = 1.0 / math.sqrt(1024)
    mixed, gtok, ggate, gup, gdown = pl.pallas_call(
        functools.partial(kernel, factor),
        name="swiglu",
        out_shape=(
            jax.ShapeDtypeStruct((16, 1024), BF),
            jax.ShapeDtypeStruct((16, 1024), BF),
            jax.ShapeDtypeStruct((128, 2048), F32),
            jax.ShapeDtypeStruct((128, 2048), F32),
            jax.ShapeDtypeStruct((256, 1024), F32),
        ),
        in_specs=[vmem] * 4,
        out_specs=[vmem] * 5,
        scratch_shapes=[
            pltpu.VMEM((2, 512, 1024), BF),
            pltpu.VMEM((1024, 1024), BF),
            pltpu.VMEM((512, 1024), BF),
            pltpu.VMEM((4, 128, 512), BF),
            pltpu.VMEM((4, 128, 512), BF),
            pltpu.VMEM((128, 512), F32),
            pltpu.VMEM((4, 128, 1024), BF),
            pltpu.VMEM((4, 128, 1024), BF),
            pltpu.VMEM((128, 1024), F32),
            pltpu.VMEM((3, 4, 128, 512), BF),
            pltpu.VMEM((1024, 512), BF),
            pltpu.VMEM((512, 512), BF),
            pltpu.VMEM((2, 4, 128, 1024), BF),
            pltpu.VMEM((2, 4, 128, 1024), BF),
            pltpu.VMEM((2, 128, 1024), F32),
            pltpu.VMEM((2, 128, 1024), F32),
            pltpu.VMEM((2, 4, 32, 1024), F32),
            pltpu.VMEM((2, 32, 1024), F32),
            pltpu.VMEM((2, 16, 1024), F32),
            pltpu.VMEM((2, 4, 128, 512), BF),
            pltpu.VMEM((2, 4, 128, 512), BF),
            pltpu.VMEM((2, 128, 512), F32),
            pltpu.VMEM((2, 4, 128, 512), BF),
            pltpu.VMEM((2, 4, 128, 512), BF),
            pltpu.VMEM((256, 1024), BF),
            pltpu.VMEM((256, 1024), BF),
            pltpu.SemaphoreType.DMA((COUNT,)),
            pltpu.SemaphoreType.DMA((COUNT,)),
        ],
        compiler_params=pltpu.CompilerParams(
            collective_id=1, has_side_effects=True, vmem_limit_bytes=48 << 20
        ),
    )(tokens, cotangent, wl, wd)

    def narrow(a):
        return jnp.concatenate([a[:, 256 * j:256 * j + unit] for j in range(8)], axis=1)

    return mixed, gtok, narrow(ggate), narrow(gup), gdown[:unit]


def solution(mesh):
    in_specs = (
        P(("gy", "gx"), "gz"),
        P(("gz", "gy"), "gx"),
        P(("gz", "gy"), "gx"),
        P(("gx", "gy"), "gz"),
        P(("gy", "gx"), "gz"),
    )
    out_specs = (
        P(("gy", "gx"), "gz"),
        P(("gy", "gx"), "gz"),
        P(("gz", "gy"), "gx"),
        P(("gz", "gy"), "gx"),
        P(("gx", "gy"), "gz"),
    )
    return jax.shard_map(body, mesh=mesh, in_specs=in_specs, out_specs=out_specs, check_vma=False)
```

```python
import functools
import math

import jax
import jax.numpy as jnp
from jax import lax
from jax.experimental import pallas as pl
from jax.experimental.pallas import tpu as pltpu
from jax.sharding import PartitionSpec as P

BF = jnp.bfloat16
F32 = jnp.float32
MESH_ID = pl.DeviceIdType.MESH
UNIT = 231


def dot_nn(a, b):
    return lax.dot_general(a, b, (((1,), (0,)), ((), ())), preferred_element_type=F32)


def dot_nt(a, b):
    return lax.dot_general(a, b, (((1,), (1,)), ((), ())), preferred_element_type=F32)


LAYOUT = {}
COUNT = 0
for name, size in (
    ("zh", 2), ("y", 6), ("x", 6), ("wx", 4), ("wc", 4), ("wd", 1),
    ("rh", 16), ("rp", 16), ("lh", 4), ("lp", 4), ("ag", 16), ("af", 4),
    ("ox", 8), ("oy", 8), ("oz", 2), ("gc", 2), ("gx", 8), ("gd", 1),
):
    LAYOUT[name] = COUNT
    COUNT += size


def kernel(
    factor,
    tok_ref, cot_ref, gw_ref, uw_ref, wd_ref,
    mixed_ref, gtok_ref, ggate_ref, gup_ref, gdown_ref,
    acts, w_loc, w, wd, parts, zs_h, zr_h, rl_h, zs_p, zr_p, rl_p, mids, tok_t, hid_t,
    o_send, o_recv, o_own, y_own, y_recv, z_send, z_recv,
    gc_send, gc_recv, g_acc, gx_send, gx_recv, gd_send, gd_recv,
    send, recv,
):
    gx, gy, z = lax.axis_index("gx"), lax.axis_index("gy"), lax.axis_index("gz")
    y, h = gx // 2, gx % 2
    x, c = gy // 2, gy % 2
    oc = 1 - c

    def at(dx=0, dc=0, dy=0, dh=0, dz=0):
        px, py, pz = (x + dx) % 4, (y + dy) % 4, (z + dz) % 4
        ph, pc = (h + dh) % 2, (c + dc) % 2
        return (py * 2 + ph, px * 2 + pc, pz)

    def copy(src, dst, who, name, s_off, r_off=None):
        r_off = s_off if r_off is None else r_off
        return pltpu.make_async_remote_copy(
            src_ref=src, dst_ref=dst,
            send_sem=send.at[LAYOUT[name] + s_off], recv_sem=recv.at[LAYOUT[name] + r_off],
            device_id=who, device_id_type=MESH_ID,
        )

    started = []
    pending = []

    def go(*args):
        cp = copy(*args)
        cp.start()
        started.append(cp)
        return cp

    def go_if(cond, *args):
        @pl.when(cond)
        def _():
            copy(*args).start()

        pending.append((cond, args))

    def wait_if(cond, *args):
        @pl.when(cond)
        def _():
            copy(*args).wait_recv()

    inner = (z == 1) | (z == 2)
    via = 1 + z // 3
    far = 3 - z
    relay_to = 3 * ((2 - z + 4) % 4 % 2)

    peers = (
        [at(dx=k) for k in (1, 2, 3)] + [at(dy=k) for k in (1, 2, 3)]
        + [at(dz=k) for k in (1, 2, 3)] + [at(dh=1), at(dc=1)]
    )
    barrier = pltpu.get_barrier_semaphore()
    for who in peers:
        pl.semaphore_signal(barrier, inc=1, device_id=who, device_id_type=MESH_ID)
    acts[0, 0:16, :] = cot_ref[...]
    acts[1, 0:16, :] = tok_ref[...]
    wd_rows = pl.ds(pl.multiple_of(c * 256, 256), 256)
    wd[wd_rows, :] = wd_ref[...]
    zeros = jnp.zeros((128, 256), BF)
    for n, ref in ((0, uw_ref), (1, gw_ref)):
        for j in range(8):
            base = n * 512 + (j % 2) * 256
            w_loc[j // 2, :, base:base + 256] = zeros
            w_loc[j // 2, :, base:base + UNIT] = ref[:, UNIT * j:UNIT * (j + 1)]
    row_own = pl.multiple_of((x * 2 + c) * 128, 128)
    w_rows = pl.ds(row_own, 128)
    w[w_rows, :] = w_loc[x]
    pl.semaphore_wait(barrier, len(peers))

    zh = [
        go((cot_ref, tok_ref)[i], acts.at[i, pl.ds(16, 16), :], at(dh=1), "zh", i) for i in (0, 1)
    ]
    wdc = go(wd_ref, wd.at[wd_rows, :], at(dc=1), "wd", 0)
    wx = {}
    for r in (1, 3, 2):
        wx[r] = go(w_loc.at[(x + r) % 4], w.at[w_rows, :], at(dx=r), "wx", r)
    wc = [go(w_loc.at[x], w.at[w_rows, :], at(dc=1), "wc", 0)]

    @pl.when(jnp.logical_not(inner))
    def _():
        zr_h[:, far] = jnp.zeros((4, 32, 512), BF)
        zr_p[:, far] = jnp.zeros((4, 32, 1024), BF)

    def spread_y(i):
        zh[i].wait_recv()
        src = acts.at[i, pl.ds(0, 32), :]
        return [
            go(src, acts.at[i, pl.ds(32 * m, 32), :], at(dy=m), "y", i * 3 + m - 1) for m in (1, 3, 2)
        ]

    def spread_x(i, copies):
        for cp in copies:
            cp.wait_recv()
        src = acts.at[i, pl.ds(0, 128), :]
        return {
            k: go(src, acts.at[i, pl.ds(128 * k, 128), :], at(dx=k), "x", i * 3 + k - 1)
            for k in (1, 3, 2)
        }

    def scatter(k, src, dst, relay, name, relay_name):
        for m in range(4):
            rows = src.at[k, pl.ds(32 * m, 32)]
            direct = (z == 1) if m == 0 else (z == 2) if m == 3 else (z != m)
            go_if(direct, rows, dst.at[k, z], (gx, gy, m), name, k * 4 + m, k * 4 + z)
            if m in (0, 3):
                go_if(z == 3 - m, rows, relay.at[k], (gx, gy, via), relay_name, k)

    def hidden_grad(k):
        def tile(j, carry):
            rows = pl.ds(pl.multiple_of(j * 256, 256), 256)
            part = dot_nt(acts[0, 128 * k:128 * (k + 1), :], wd[rows, :])
            zs_h[k, :, rows] = part.astype(BF)
            parts[k, :, pl.ds(pl.multiple_of(j * 256 + 1024, 256), 256)] = part
            return carry

        lax.fori_loop(0, 2, tile, 0)
        scatter(k, zs_h, zr_h, rl_h, "rh", "lh")

    def gate_up(k):
        def tile(j, carry):
            cols = pl.ds(pl.multiple_of(j * 256, 256), 256)
            part = dot_nn(acts[1, 128 * k:128 * (k + 1), :], w[:, cols])
            zs_p[k, :, cols] = part.astype(BF)
            parts[k, :, cols] = part
            return carry

        lax.fori_loop(0, 4, tile, 0)
        scatter(k, zs_p, zr_p, rl_p, "rp", "lp")

    def relay(k):
        rows = pl.ds(pl.multiple_of(relay_to * 32, 32), 32)

        @pl.when(inner)
        def _():
            copy(rl_h.at[k], rl_h.at[k], (gx, gy, 3 - relay_to), "lh", k).wait_recv()
            zs_h[k, rows, :] = (parts[k, rows, 1024:1536] + rl_h[k].astype(F32)).astype(BF)
            copy(rl_p.at[k], rl_p.at[k], (gx, gy, 3 - relay_to), "lp", k).wait_recv()
            zs_p[k, rows, :] = (parts[k, rows, 0:1024] + rl_p[k].astype(F32)).astype(BF)

        for m in (0, 3):
            sel = z == (2 if m == 0 else 1)
            piece = pl.ds(32 * m, 32)
            go_if(sel, zs_h.at[k, piece], zr_h.at[k, z], (gx, gy, m), "rh", k * 4 + m, k * 4 + z)
            go_if(sel, zs_p.at[k, piece], zr_p.at[k, z], (gx, gy, m), "rp", k * 4 + m, k * 4 + z)

    def mix(k):
        for s in range(4):
            cond = (z != s) & (z != 3 - s) if s in (0, 3) else z != s
            wait_if(cond, zs_h.at[k, pl.ds(0, 32)], zr_h.at[k, s], (gx, gy, s), "rh", k * 4 + s)
            wait_if(cond, zs_p.at[k, pl.ds(0, 32)], zr_p.at[k, s], (gx, gy, s), "rp", k * 4 + s)
        mine = pl.ds(pl.multiple_of(z * 32, 32), 32)
        out = pl.ds(pl.multiple_of(z * 32 + 128 * k, 32), 32)

        def tile(j, carry):
            def total(got, off, skip):
                here = pl.ds(pl.multiple_of(j * 128 + off, 128), 128)
                mid = pl.ds(pl.multiple_of(j * 128 + off + skip, 128), 128)
                return (
                    (parts[k, mine, mid] + got[k, (z + 1) % 4, :, here].astype(F32))
                    + (got[k, (z + 2) % 4, :, here].astype(F32) + got[k, (z + 3) % 4, :, here].astype(F32))
                )

            up = total(zr_p, 0, 0)
            gate = total(zr_p, 512, 0)
            grad = total(zr_h, 0, 1024)
            sigma = jax.nn.sigmoid(gate)
            swish = gate * sigma

            def put(n, value):
                mids[out, pl.ds(pl.multiple_of(j * 128 + 512 * n, 128), 128)] = value.astype(BF)

            put(0, grad * swish)
            put(1, grad * up * sigma * (1.0 + gate * (1.0 - sigma)))
            put(2, swish * up)
            return carry

        lax.fori_loop(0, 4, tile, 0)
        block = mids.at[out, :]
        for m in range(4):
            cond = (z != m) & (z != 3 - m) if m in (0, 3) else z != m
            go_if(cond, block, block, (gx, gy, m), "ag", k * 4 + m, k * 4 + z)

    def forward(k):
        for m in (0, 3):
            sel = z == (1 if m == 0 else 2)
            block = mids.at[pl.ds(128 * k + 32 * (3 - m), 32), :]
            wait_if(sel, block, block, (gx, gy, 3 - m), "ag", k * 4 + 3 - m)
            go_if(sel, block, block, (gx, gy, m), "af", k, k * 4 - LAYOUT["af"] + LAYOUT["ag"] + 3 - m)

    def arrived(k):
        for s in range(4):
            cond = z != s
            if s == 0:
                cond = cond & (z != 2)
            if s == 3:
                cond = cond & (z != 1)
            block = mids.at[pl.ds(128 * k + 32 * s, 32), :]
            wait_if(cond, block, block, (gx, gy, s), "ag", k * 4 + s)

    def out_block(n, k):
        slot = pl.ds(128 * k, 128)

        def tile(j, carry):
            cols = pl.ds(pl.multiple_of(j * 256, 256), 256)
            if n == 0:
                part = dot_nt(mids[slot, 0:1024], w[cols, :])
            else:
                part = dot_nn(mids[slot, 1024:1536], wd[:, cols])
            if k:
                o_send[n, k, :, cols] = part.astype(BF)
            else:
                o_own[n, :, cols] = part
            return carry

        lax.fori_loop(0, 4, tile, 0)
        if k:
            go(o_send.at[n, k], o_recv.at[n, k], at(dx=4 - k), "ox", n * 4 + k)

    def project(k):
        arrived(k)
        out_block(0, k)
        out_block(1, k)

    cot_y = spread_y(0)
    tok_y = spread_y(1)
    cot_x = spread_x(0, cot_y)
    wdc.wait_recv()
    hidden_grad(0)
    for r in (1, 3, 2):
        wx[r].wait_recv()
        rows = pl.ds(pl.multiple_of(((x - r + 4) % 4 * 2 + c) * 128, 128), 128)
        wc.append(go(w.at[rows, :], w.at[rows, :], at(dc=1), "wc", r))
    tok_x = spread_x(1, tok_y)
    for cp in wc:
        cp.wait_recv()
    gate_up(0)
    for k in (1, 3, 2):
        cot_x[k].wait_recv()
        hidden_grad(k)
    relay(0)
    mix(0)
    tok_x[1].wait_recv()
    gate_up(1)
    forward(0)
    tok_x[3].wait_recv()
    gate_up(3)
    relay(1)
    mix(1)
    tok_x[2].wait_recv()
    gate_up(2)
    relay(3)
    forward(1)
    project(0)
    mix(3)
    relay(2)
    forward(3)
    project(1)
    mix(2)

    for j in range(8):
        tok_t[j % 2, 128 * (j // 2):128 * (j // 2 + 1), :] = acts[1, :, 128 * j:128 * (j + 1)].T

    forward(2)
    project(3)
    project(2)

    def grads(n, mine):
        side = c if mine else oc

        def tile(j, carry):
            cols = pl.ds(pl.multiple_of(j * 256, 256), 256)
            source = pl.ds(pl.multiple_of(j * 256 + 512 * n, 256), 256)
            part = dot_nn(tok_t[side], mids[:, source]) * factor
            if mine:
                g_acc[n, :, cols] = part
            else:
                gc_send[n, :, cols] = part.astype(BF)
            return carry

        lax.fori_loop(0, 2, tile, 0)

    def spread_grads(n, cp):
        cp.wait_recv()
        for r in (1, 3, 2):
            to = (x + r) % 4
            rows = pl.ds(pl.multiple_of(to * 128, 128), 128)
            gx_send[n, r] = (g_acc[n, rows, :] + gc_recv[n, rows, :].astype(F32)).astype(BF)
            go(gx_send.at[n, r], gx_recv.at[n, x], at(dx=r), "gx", n * 4 + r)
        rows = pl.ds(pl.multiple_of(x * 128, 128), 128)
        g_acc[n, rows, :] = g_acc[n, rows, :] + gc_recv[n, rows, :].astype(F32)

    grads(0, False)
    gc0 = go(gc_send.at[0], gc_recv.at[0], at(dc=1), "gc", 0)
    grads(1, False)
    gc1 = go(gc_send.at[1], gc_recv.at[1], at(dc=1), "gc", 1)
    grads(0, True)
    spread_grads(0, gc0)
    grads(1, True)
    spread_grads(1, gc1)

    for k in range(4):
        hid_t[:, 128 * k:128 * (k + 1)] = mids[128 * k:128 * (k + 1), 1024:1536].T
    theirs = pl.ds(pl.multiple_of(oc * 256, 256), 256)

    def down_theirs(j, carry):
        cols = pl.ds(pl.multiple_of(j * 256, 256), 256)
        gd_send[:, cols] = (dot_nn(hid_t[theirs, :], acts[0, :, cols]) * factor).astype(BF)
        return carry

    lax.fori_loop(0, 4, down_theirs, 0)
    gd = go(gd_send, gd_recv, at(dc=1), "gd", 0)

    oy = {}
    for n in (0, 1):
        for k in (1, 2, 3):
            copy(o_send.at[n, k], o_recv.at[n, k], at(dx=4 - k), "ox", n * 4 + k).wait_recv()
        y_own[n] = (o_own[n] + o_recv[n, 1].astype(F32)) + (
            o_recv[n, 2].astype(F32) + o_recv[n, 3].astype(F32)
        )
        for m in (1, 3, 2):
            oy[n, m] = go(
                y_own.at[n, pl.ds(32 * m, 32), :], y_recv.at[n, m], at(dy=4 - m), "oy", n * 4 + m
            )

    def down_ours(j, carry):
        cols = pl.ds(pl.multiple_of(j * 256, 256), 256)
        gdown_ref[:, cols] = dot_nn(hid_t[wd_rows, :], acts[0, :, cols]) * factor
        return carry

    lax.fori_loop(0, 4, down_ours, 0)
    gd.wait_recv()
    gdown_ref[...] += gd_recv[...].astype(F32)

    oz = []
    for n in (0, 1):
        for m in (1, 2, 3):
            oy[n, m].wait_recv()
        z_send[n] = (y_own[n, 0:32, :] + y_recv[n, 1]) + (y_recv[n, 2] + y_recv[n, 3])
        oz.append(go(z_send.at[n, pl.ds(16, 16), :], z_recv.at[n], at(dh=1), "oz", n))

    for n, out in ((0, gup_ref), (1, ggate_ref)):
        for r in (1, 2, 3):
            slot = (x - r + 4) % 4
            copy(gx_send.at[n, r], gx_recv.at[n, slot], at(dx=r), "gx", n * 4 + r).wait_recv()
        rows = pl.ds(pl.multiple_of(x * 128, 128), 128)
        for p in range(4):
            for j in (0, 1):
                cols = slice(256 * j, 256 * j + UNIT)
                to = slice(UNIT * (2 * p + j), UNIT * (2 * p + j + 1))

                @pl.when(x == p)
                def _():
                    out[:, to] = g_acc[n, rows, cols]

                @pl.when(x != p)
                def _():
                    out[:, to] = gx_recv[n, p, :, cols].astype(F32)

    for n, out in ((0, gtok_ref), (1, mixed_ref)):
        oz[n].wait_recv()
        out[...] = (z_send[n, 0:16, :] + z_recv[n]).astype(BF)

    for cp in started:
        cp.wait_send()
    for cond, args in pending:
        @pl.when(cond)
        def _():
            copy(*args).wait_send()


def body(tokens, gate_weight, up_weight, down_weight, cotangent):
    wd = jnp.pad(down_weight, ((0, 256 - UNIT), (0, 0)))
    vmem = pl.BlockSpec(memory_space=pltpu.VMEM)
    factor = 1.0 / math.sqrt(1024)
    mixed, gtok, ggate, gup, gdown = pl.pallas_call(
        functools.partial(kernel, factor),
        name="swiglu",
        out_shape=(
            jax.ShapeDtypeStruct((16, 1024), BF),
            jax.ShapeDtypeStruct((16, 1024), BF),
            jax.ShapeDtypeStruct((128, 1848), F32),
            jax.ShapeDtypeStruct((128, 1848), F32),
            jax.ShapeDtypeStruct((256, 1024), F32),
        ),
        in_specs=[vmem] * 5,
        out_specs=[vmem] * 5,
        scratch_shapes=[
            pltpu.VMEM((2, 512, 1024), BF),
            pltpu.VMEM((4, 128, 1024), BF),
            pltpu.VMEM((1024, 1024), BF),
            pltpu.VMEM((512, 1024), BF),
            pltpu.VMEM((4, 128, 1536), F32),
            pltpu.VMEM((4, 128, 512), BF),
            pltpu.VMEM((4, 4, 32, 512), BF),
            pltpu.VMEM((4, 32, 512), BF),
            pltpu.VMEM((4, 128, 1024), BF),
            pltpu.VMEM((4, 4, 32, 1024), BF),
            pltpu.VMEM((4, 32, 1024), BF),
            pltpu.VMEM((512, 1536), BF),
            pltpu.VMEM((2, 512, 512), BF),
            pltpu.VMEM((512, 512), BF),
            pltpu.VMEM((2, 4, 128, 1024), BF),
            pltpu.VMEM((2, 4, 128, 1024), BF),
            pltpu.VMEM((2, 128, 1024), F32),
            pltpu.VMEM((2, 128, 1024), F32),
            pltpu.VMEM((2, 4, 32, 1024), F32),
            pltpu.VMEM((2, 32, 1024), F32),
            pltpu.VMEM((2, 16, 1024), F32),
            pltpu.VMEM((2, 512, 512), BF),
            pltpu.VMEM((2, 512, 512), BF),
            pltpu.VMEM((2, 512, 512), F32),
            pltpu.VMEM((2, 4, 128, 512), BF),
            pltpu.VMEM((2, 4, 128, 512), BF),
            pltpu.VMEM((256, 1024), BF),
            pltpu.VMEM((256, 1024), BF),
            pltpu.SemaphoreType.DMA((COUNT,)),
            pltpu.SemaphoreType.DMA((COUNT,)),
        ],
        compiler_params=pltpu.CompilerParams(
            collective_id=1, has_side_effects=True, vmem_limit_bytes=48 << 20
        ),
    )(tokens, cotangent, gate_weight, up_weight, wd)
    return mixed, gtok, ggate, gup, gdown[:UNIT]


def solution(mesh):
    in_specs = (
        P(("gy", "gx"), "gz"),
        P(("gz", "gy"), "gx"),
        P(("gz", "gy"), "gx"),
        P(("gx", "gy"), "gz"),
        P(("gy", "gx"), "gz"),
    )
    out_specs = (
        P(("gy", "gx"), "gz"),
        P(("gy", "gx"), "gz"),
        P(("gz", "gy"), "gx"),
        P(("gz", "gy"), "gx"),
        P(("gx", "gy"), "gz"),
    )
    return jax.shard_map(body, mesh=mesh, in_specs=in_specs, out_specs=out_specs, check_vma=False)
```

```python
import functools
import math

import jax
import jax.numpy as jnp
from jax import lax
from jax.experimental import pallas as pl
from jax.experimental.pallas import tpu as pltpu
from jax.sharding import PartitionSpec as P

BF = jnp.bfloat16
F32 = jnp.float32
ORDER = "H1 P1 R0 H3 P3 D0 H2 P2 R1 R3 F0 D1 R2 D3 F1 G0 D2 F3 G1 F2 G3 G2"
MESH_ID = pl.DeviceIdType.MESH
UNIT = 231


def dot_nn(a, b):
    return lax.dot_general(a, b, (((1,), (0,)), ((), ())), preferred_element_type=F32)


def dot_nt(a, b):
    return lax.dot_general(a, b, (((1,), (1,)), ((), ())), preferred_element_type=F32)


LAYOUT = {}
COUNT = 0
for name, size in (
    ("zh", 2), ("y", 6), ("x", 6), ("x1", 6), ("y2", 6), ("wx", 4), ("wc", 4), ("wd", 1),
    ("rh", 16), ("rp", 16), ("lh", 4), ("lp", 4), ("ag", 16), ("af", 4),
    ("ox", 8), ("oy", 8), ("oz", 2), ("py", 32), ("px", 8), ("gc", 4), ("gx", 4), ("gd", 1),
):
    LAYOUT[name] = COUNT
    COUNT += size


def kernel(
    factor,
    tok_ref, cot_ref, gw_ref, uw_ref, wd_ref,
    mixed_ref, gtok_ref, ggate_ref, gup_ref, gdown_ref,
    acts, w_loc, w, wd, parts, zs_h, zr_h, rl_h, zs_p, zr_p, rl_p, mids, mids_t, tok_in, cot_in, wd_in, wd_own,
    o_send, o_recv, o_own, p_own, p_recv, p_sum, px_recv, y_own, y_recv, z_send, z_recv,
    gc_send, gc_recv, g_acc, g_out, gx_send, gx_recv, gd_send, gd_recv, gd_own,
    send, recv, local,
):
    gx, gy, z = lax.axis_index("gx"), lax.axis_index("gy"), lax.axis_index("gz")
    y, h = gx // 2, gx % 2
    x, c = gy // 2, gy % 2
    oc = 1 - c

    def at(dx=0, dc=0, dy=0, dh=0, dz=0):
        px, py, pz = (x + dx) % 4, (y + dy) % 4, (z + dz) % 4
        ph, pc = (h + dh) % 2, (c + dc) % 2
        return (py * 2 + ph, px * 2 + pc, pz)

    def copy(src, dst, who, name, s_off, r_off=None):
        r_off = s_off if r_off is None else r_off
        return pltpu.make_async_remote_copy(
            src_ref=src, dst_ref=dst,
            send_sem=send.at[LAYOUT[name] + s_off], recv_sem=recv.at[LAYOUT[name] + r_off],
            device_id=who, device_id_type=MESH_ID,
        )

    started = []
    pending = []

    def go(*args):
        cp = copy(*args)
        cp.start()
        started.append(cp)
        return cp

    def go_if(cond, *args):
        @pl.when(cond)
        def _():
            copy(*args).start()

        pending.append((cond, args))

    def wait_if(cond, *args):
        @pl.when(cond)
        def _():
            copy(*args).wait_recv()

    inner = (z == 1) | (z == 2)
    via = 1 + z // 3
    far = 3 - z
    relay_to = 3 * ((2 - z + 4) % 4 % 2)

    peers = (
        [at(dx=k) for k in (1, 2, 3)] + [at(dy=k) for k in (1, 2, 3)]
        + [at(dz=k) for k in (1, 2, 3)] + [at(dh=1), at(dc=1)]
    )
    loads = [
        pltpu.make_async_copy(src, dst, local.at[i])
        for i, (src, dst) in enumerate(((cot_ref, cot_in), (tok_ref, tok_in), (wd_ref, wd_in)))
    ]
    for load in loads:
        load.start()
    barrier = pltpu.get_barrier_semaphore()
    for who in peers:
        pl.semaphore_signal(barrier, inc=1, device_id=who, device_id_type=MESH_ID)
    zeros = jnp.zeros((128, 256), BF)
    for n, ref in ((0, uw_ref), (1, gw_ref)):
        for j in range(8):
            base = n * 512 + (j % 2) * 256
            w_loc[j // 2, :, base:base + 256] = zeros
            w_loc[j // 2, :, base:base + UNIT] = ref[:, UNIT * j:UNIT * (j + 1)]
    row_own = pl.multiple_of((x * 2 + c) * 128, 128)
    w_rows = pl.ds(row_own, 128)
    w[w_rows, :] = w_loc[x]
    for load in loads:
        load.wait()
    acts[0, 0, 0, 0:16, :] = cot_in[...]
    acts[1, 0, 0, 0:16, :] = tok_in[...]
    wd_rows = pl.ds(pl.multiple_of(c * 256, 256), 256)
    wd_own[224:256, :] = jnp.zeros((32, 1024), BF)
    wd_own[0:UNIT, :] = wd_in[...]
    wd[wd_rows, :] = wd_own[...]
    pl.semaphore_wait(barrier, len(peers))

    zh = [
        go((cot_in, tok_in)[i], acts.at[i, 0, 0, pl.ds(16, 16), :], at(dh=1), "zh", i) for i in (0, 1)
    ]
    wdc = go(wd_own, wd.at[wd_rows, :], at(dc=1), "wd", 0)
    wx = {}
    for r in (1, 3, 2):
        wx[r] = go(w_loc.at[(x + r) % 4], w.at[w_rows, :], at(dx=r), "wx", r)
    wc = [go(w_loc.at[x], w.at[w_rows, :], at(dc=1), "wc", 0)]

    @pl.when(jnp.logical_not(inner))
    def _():
        zr_h[:, far] = jnp.zeros((4, 32, 512), BF)
        zr_p[:, far] = jnp.zeros((4, 32, 1024), BF)

    low, high = pl.ds(0, 512), pl.ds(512, 512)

    def spread_own(i):
        zh[i].wait_recv()
        src = acts.at[i, 0, 0]
        over_y = [go(src, acts.at[i, 0, m], at(dy=m), "y", i * 3 + m - 1) for m in (1, 3, 2)]
        over_x = [
            go(src.at[:, high], acts.at[i, k, 0, :, high], at(dx=k), "x1", i * 3 + k - 1)
            for k in (1, 3, 2)
        ]
        return over_y, over_x

    def spread_x(i, ks):
        for k in ks:
            src, dst = acts.at[i, 0, :, :, low], acts.at[i, k, :, :, low]
            slots[i, k] = go(src, dst, at(dx=k), "x", i * 3 + k - 1)

    def spread_y(i, copies):
        for cp in copies:
            cp.wait_recv()
        out = []
        for m in (1, 3, 2):
            src, dst = acts.at[i, pl.ds(1, 3), 0, :, high], acts.at[i, pl.ds(1, 3), m, :, high]
            out.append(go(src, dst, at(dy=m), "y2", i * 3 + m - 1))
        rights[i] = out

    def slot_ready(i, k):
        for cp in rights[i]:
            cp.wait_recv()
        rights[i] = []
        slots[i, k].wait_recv()

    slots, rights = {}, {}

    def scatter(k, src, dst, relay, name, relay_name):
        for m in range(4):
            rows = src.at[k, pl.ds(32 * m, 32)]
            direct = (z == 1) if m == 0 else (z == 2) if m == 3 else (z != m)
            go_if(direct, rows, dst.at[k, z], (gx, gy, m), name, k * 4 + m, k * 4 + z)
            if m in (0, 3):
                go_if(z == 3 - m, rows, relay.at[k], (gx, gy, via), relay_name, k)

    def hidden_grad(k):
        def tile(j, carry):
            rows = pl.ds(pl.multiple_of(j * 256, 256), 256)
            part = dot_nt(acts[0, k].reshape(128, 1024), wd[rows, :])
            zs_h[k, :, rows] = part.astype(BF)
            parts[k, :, pl.ds(pl.multiple_of(j * 256 + 1024, 256), 256)] = part
            return carry

        lax.fori_loop(0, 2, tile, 0, unroll=True)
        scatter(k, zs_h, zr_h, rl_h, "rh", "lh")

    def gate_up(k):
        def tile(j, carry):
            cols = pl.ds(pl.multiple_of(j * 256, 256), 256)
            part = dot_nn(acts[1, k].reshape(128, 1024), w[:, cols])
            zs_p[k, :, cols] = part.astype(BF)
            parts[k, :, cols] = part
            return carry

        lax.fori_loop(0, 4, tile, 0, unroll=True)
        scatter(k, zs_p, zr_p, rl_p, "rp", "lp")

    def relay(k):
        rows = pl.ds(pl.multiple_of(relay_to * 32, 32), 32)

        @pl.when(inner)
        def _():
            copy(rl_h.at[k], rl_h.at[k], (gx, gy, 3 - relay_to), "lh", k).wait_recv()
            zs_h[k, rows, :] = (parts[k, rows, 1024:1536] + rl_h[k].astype(F32)).astype(BF)
            copy(rl_p.at[k], rl_p.at[k], (gx, gy, 3 - relay_to), "lp", k).wait_recv()
            zs_p[k, rows, :] = (parts[k, rows, 0:1024] + rl_p[k].astype(F32)).astype(BF)

        for m in (0, 3):
            sel = z == (2 if m == 0 else 1)
            piece = pl.ds(32 * m, 32)
            go_if(sel, zs_h.at[k, piece], zr_h.at[k, z], (gx, gy, m), "rh", k * 4 + m, k * 4 + z)
            go_if(sel, zs_p.at[k, piece], zr_p.at[k, z], (gx, gy, m), "rp", k * 4 + m, k * 4 + z)

    def mix(k):
        for s in range(4):
            cond = (z != s) & (z != 3 - s) if s in (0, 3) else z != s
            wait_if(cond, zs_h.at[k, pl.ds(0, 32)], zr_h.at[k, s], (gx, gy, s), "rh", k * 4 + s)
            wait_if(cond, zs_p.at[k, pl.ds(0, 32)], zr_p.at[k, s], (gx, gy, s), "rp", k * 4 + s)
        mine = pl.ds(pl.multiple_of(z * 32, 32), 32)
        out = pl.ds(pl.multiple_of(z * 32 + 128 * k, 32), 32)

        def tile(j, carry):
            def total(got, off, skip):
                here = pl.ds(pl.multiple_of(j * 128 + off, 128), 128)
                mid = pl.ds(pl.multiple_of(j * 128 + off + skip, 128), 128)
                return (
                    (parts[k, mine, mid] + got[k, (z + 1) % 4, :, here].astype(F32))
                    + (got[k, (z + 2) % 4, :, here].astype(F32) + got[k, (z + 3) % 4, :, here].astype(F32))
                )

            up = total(zr_p, 0, 0)
            gate = total(zr_p, 512, 0)
            grad = total(zr_h, 0, 1024)
            sigma = jax.nn.sigmoid(gate)
            swish = gate * sigma

            def put(n, value):
                mids[out, pl.ds(pl.multiple_of(j * 128 + 512 * n, 128), 128)] = value.astype(BF)

            put(0, grad * swish)
            put(1, grad * up * sigma * (1.0 + gate * (1.0 - sigma)))
            put(2, swish * up)
            return carry

        lax.fori_loop(0, 4, tile, 0, unroll=True)
        block = mids.at[out, :]
        for m in range(4):
            cond = (z != m) & (z != 3 - m) if m in (0, 3) else z != m
            go_if(cond, block, block, (gx, gy, m), "ag", k * 4 + m, k * 4 + z)

    def forward(k):
        for m in (0, 3):
            sel = z == (1 if m == 0 else 2)
            block = mids.at[pl.ds(128 * k + 32 * (3 - m), 32), :]
            wait_if(sel, block, block, (gx, gy, 3 - m), "ag", k * 4 + 3 - m)
            go_if(sel, block, block, (gx, gy, m), "af", k, k * 4 - LAYOUT["af"] + LAYOUT["ag"] + 3 - m)

    def arrived(k):
        for s in range(4):
            cond = z != s
            if s == 0:
                cond = cond & (z != 2)
            if s == 3:
                cond = cond & (z != 1)
            block = mids.at[pl.ds(128 * k + 32 * s, 32), :]
            wait_if(cond, block, block, (gx, gy, s), "ag", k * 4 + s)

    def out_block(n, k):
        slot = pl.ds(128 * k, 128)

        def tile(j):
            cols = slice(256 * j, 256 * (j + 1))
            if n == 0:
                part = dot_nt(mids[slot, 0:1024], w[cols, :])
            else:
                part = dot_nn(mids[slot, 1024:1536], wd[:, cols])
            if k or j >= 2:
                o_send[n, k, :, cols] = part.astype(BF)
            if k == 0:
                o_own[n, :, cols] = part
            elif j >= 2:
                p_own[n, k, :, 256 * (j - 2):256 * (j - 1)] = part[0:32]

        for j in range(4):
            tile(j)
        if k:
            go(o_send.at[n, k, :, low], o_recv.at[n, k], at(dx=4 - k), "ox", n * 4 + k)
        for m in (1, 3, 2):
            src = o_send.at[n, k, pl.ds(32 * m, 32), high]
            go(src, p_recv.at[n, k, m], at(dy=4 - m), "py", n * 16 + k * 4 + m)

    def slot_cols(k):
        return slice(128 * k, 128 * (k + 1))

    def project(k):
        arrived(k)
        out_block(0, k)
        out_block(1, k)
        for j in range(12):
            mids_t[128 * j:128 * (j + 1), slot_cols(k)] = mids[slot_cols(k), 128 * j:128 * (j + 1)].T

    cot_y, cot_x = spread_own(0)
    tok_y, tok_x = spread_own(1)
    for cp in cot_y:
        cp.wait_recv()
    spread_x(0, (1, 3))
    wdc.wait_recv()
    hidden_grad(0)
    for cp in tok_y:
        cp.wait_recv()
    spread_x(1, (1, 3))
    spread_y(0, cot_x)
    spread_y(1, tok_x)
    for r in (1, 3, 2):
        wx[r].wait_recv()
        rows = pl.ds(pl.multiple_of(((x - r + 4) % 4 * 2 + c) * 128, 128), 128)
        wc.append(go(w.at[rows, :], w.at[rows, :], at(dc=1), "wc", r))
    spread_x(0, (2,))
    spread_x(1, (2,))
    for cp in wc:
        cp.wait_recv()
    gate_up(0)

    def slot_h(k):
        slot_ready(0, k)
        hidden_grad(k)

    def slot_p(k):
        slot_ready(1, k)
        gate_up(k)

    steps = {"H": slot_h, "P": slot_p, "R": relay, "D": mix, "F": forward, "G": project}
    for step in ORDER.split():
        steps[step[0]](int(step[1]))

    early = list(started), list(pending)
    del started[:], pending[:]

    def drain(copies, conds):
        for cp in copies:
            cp.wait_send()
        for cond, args in conds:
            @pl.when(cond)
            def _():
                copy(*args).wait_send()

    def token_cols(to, side):
        cols = pl.ds(pl.multiple_of((to * 2 + side) * 128, 128), 128)
        return acts[1, :, :, :, cols].reshape(512, 128)

    gc = {}
    for r in (1, 3, 2, 0):
        to = (x + r) % 4
        both = jnp.concatenate([token_cols(to, oc), token_cols(to, c)], axis=1)
        for n in range(4):
            part = dot_nn(mids_t[256 * n:256 * (n + 1)], both) * factor
            gc_send[r, 256 * n:256 * (n + 1), :] = part[:, 0:128].astype(BF)
            g_acc[r, 256 * n:256 * (n + 1), :] = part[:, 128:256]
        gc[r] = go(gc_send.at[r], gc_recv.at[r], at(dc=1), "gc", r)
    for r in (1, 3, 2):
        gc[r].wait_recv()
        gx_send[r] = (g_acc[r] + gc_recv[r].astype(F32)).astype(BF)
        go(gx_send.at[r], gx_recv.at[x], at(dx=r), "gx", r)

    drain(*early)
    theirs = pl.ds(pl.multiple_of(oc * 256 + 1024, 256), 256)
    ours = pl.ds(pl.multiple_of(c * 256 + 1024, 256), 256)

    def down_theirs(j, carry):
        cols = pl.ds(pl.multiple_of(j * 256, 256), 256)
        gd_send[:, cols] = (dot_nn(mids_t[theirs, :], acts[0, :, :, :, cols].reshape(512, 256)) * factor).astype(BF)
        return carry

    lax.fori_loop(0, 4, down_theirs, 0, unroll=True)
    gd = go(gd_send, gd_recv, at(dc=1), "gd", 0)

    oy, px = {}, {}
    for n in (0, 1):
        for k in range(4):
            for m in (1, 2, 3):
                src = o_send.at[n, k, pl.ds(32 * m, 32), high]
                copy(src, p_recv.at[n, k, m], at(dy=4 - m), "py", n * 16 + k * 4 + m).wait_recv()
            mine = p_own[n, k] if k else o_own[n, 0:32, 512:1024]
            p_sum[n, k] = (mine + p_recv[n, k, 1].astype(F32)) + (
                p_recv[n, k, 2].astype(F32) + p_recv[n, k, 3].astype(F32)
            )
            if k:
                px[n, k] = go(p_sum.at[n, k], px_recv.at[n, k], at(dx=4 - k), "px", n * 4 + k)
        for k in (1, 2, 3):
            src = o_send.at[n, k, :, low]
            copy(src, o_recv.at[n, k], at(dx=4 - k), "ox", n * 4 + k).wait_recv()
        y_own[n] = (o_own[n, :, 0:512] + o_recv[n, 1].astype(F32)) + (
            o_recv[n, 2].astype(F32) + o_recv[n, 3].astype(F32)
        )
        for m in (1, 3, 2):
            oy[n, m] = go(
                y_own.at[n, pl.ds(32 * m, 32), :], y_recv.at[n, m], at(dy=4 - m), "oy", n * 4 + m
            )

    def down_ours(j, carry):
        cols = pl.ds(pl.multiple_of(j * 256, 256), 256)
        gd_own[:, cols] = dot_nn(mids_t[ours, :], acts[0, :, :, :, cols].reshape(512, 256)) * factor
        return carry

    lax.fori_loop(0, 4, down_ours, 0, unroll=True)
    gd.wait_recv()
    gdown_ref[...] = gd_own[0:UNIT, :] + gd_recv[0:UNIT, :].astype(F32)

    oz = []
    for n in (0, 1):
        for m in (1, 2, 3):
            oy[n, m].wait_recv()
        z_send[n, :, 0:512] = (y_own[n, 0:32, :] + y_recv[n, 1]) + (y_recv[n, 2] + y_recv[n, 3])
        for k in (1, 2, 3):
            px[n, k].wait_recv()
        z_send[n, :, 512:1024] = (p_sum[n, 0] + px_recv[n, 1]) + (px_recv[n, 2] + px_recv[n, 3])
        oz.append(go(z_send.at[n, pl.ds(16, 16), :], z_recv.at[n], at(dh=1), "oz", n))

    gc[0].wait_recv()
    for r in (1, 2, 3):
        slot = (x - r + 4) % 4
        copy(gx_send.at[r], gx_recv.at[slot], at(dx=r), "gx", r).wait_recv()
    for p in range(4):
        @pl.when(x == p)
        def _():
            g_out[...] = g_acc[0] + gc_recv[0].astype(F32)

        @pl.when(x != p)
        def _():
            g_out[...] = gx_recv[p].astype(F32)

        for n, out in ((0, gup_ref), (1, ggate_ref)):
            for j in (0, 1):
                row = UNIT * (2 * p + j)
                out[row:row + UNIT, :] = g_out[512 * n + 256 * j:512 * n + 256 * j + UNIT, :]

    for n, out in ((0, gtok_ref), (1, mixed_ref)):
        oz[n].wait_recv()
        out[...] = (z_send[n, 0:16, :] + z_recv[n]).astype(BF)

    drain(started, pending)


def write_out(*refs):
    sems = refs[10]
    copies = [pltpu.make_async_copy(refs[i], refs[5 + i], sems.at[i]) for i in range(5)]
    for cp in copies:
        cp.start()
    for cp in copies:
        cp.wait()


def body(tokens, gate_weight, up_weight, down_weight, cotangent):
    vmem = pl.BlockSpec(memory_space=pltpu.VMEM)
    factor = 1.0 / math.sqrt(1024)
    anywhere = pl.BlockSpec(memory_space=pl.ANY)
    results = pl.pallas_call(
        functools.partial(kernel, factor),
        name="swiglu",
        out_shape=(
            jax.ShapeDtypeStruct((16, 1024), BF),
            jax.ShapeDtypeStruct((16, 1024), BF),
            jax.ShapeDtypeStruct((1848, 128), F32),
            jax.ShapeDtypeStruct((1848, 128), F32),
            jax.ShapeDtypeStruct((UNIT, 1024), F32),
        ),
        in_specs=[anywhere, anywhere, vmem, vmem, anywhere],
        out_specs=[vmem] * 5,
        scratch_shapes=[
            pltpu.VMEM((2, 4, 4, 32, 1024), BF),
            pltpu.VMEM((4, 128, 1024), BF),
            pltpu.VMEM((1024, 1024), BF),
            pltpu.VMEM((512, 1024), BF),
            pltpu.VMEM((4, 128, 1536), F32),
            pltpu.VMEM((4, 128, 512), BF),
            pltpu.VMEM((4, 4, 32, 512), BF),
            pltpu.VMEM((4, 32, 512), BF),
            pltpu.VMEM((4, 128, 1024), BF),
            pltpu.VMEM((4, 4, 32, 1024), BF),
            pltpu.VMEM((4, 32, 1024), BF),
            pltpu.VMEM((512, 1536), BF),
            pltpu.VMEM((1536, 512), BF),
            pltpu.VMEM((16, 1024), BF),
            pltpu.VMEM((16, 1024), BF),
            pltpu.VMEM((UNIT, 1024), BF),
            pltpu.VMEM((256, 1024), BF),
            pltpu.VMEM((2, 4, 128, 1024), BF),
            pltpu.VMEM((2, 4, 128, 512), BF),
            pltpu.VMEM((2, 128, 1024), F32),
            pltpu.VMEM((2, 4, 32, 512), F32),
            pltpu.VMEM((2, 4, 4, 32, 512), BF),
            pltpu.VMEM((2, 4, 32, 512), F32),
            pltpu.VMEM((2, 4, 32, 512), F32),
            pltpu.VMEM((2, 128, 512), F32),
            pltpu.VMEM((2, 4, 32, 512), F32),
            pltpu.VMEM((2, 32, 1024), F32),
            pltpu.VMEM((2, 16, 1024), F32),
            pltpu.VMEM((4, 1024, 128), BF),
            pltpu.VMEM((4, 1024, 128), BF),
            pltpu.VMEM((4, 1024, 128), F32),
            pltpu.VMEM((1024, 128), F32),
            pltpu.VMEM((4, 1024, 128), BF),
            pltpu.VMEM((4, 1024, 128), BF),
            pltpu.VMEM((256, 1024), BF),
            pltpu.VMEM((256, 1024), BF),
            pltpu.VMEM((256, 1024), F32),
            pltpu.SemaphoreType.DMA((COUNT,)),
            pltpu.SemaphoreType.DMA((COUNT,)),
            pltpu.SemaphoreType.DMA((3,)),
        ],
        compiler_params=pltpu.CompilerParams(
            collective_id=1, has_side_effects=True, vmem_limit_bytes=48 << 20
        ),
    )(tokens, cotangent, gate_weight, up_weight, down_weight)
    mixed, gtok, ggate, gup, gdown = pl.pallas_call(
        write_out,
        name="write_out",
        out_shape=tuple(jax.ShapeDtypeStruct(a.shape, a.dtype) for a in results),
        in_specs=[vmem] * 5,
        out_specs=[anywhere] * 5,
        scratch_shapes=[pltpu.SemaphoreType.DMA((5,))],
        compiler_params=pltpu.CompilerParams(vmem_limit_bytes=16 << 20),
    )(*results)
    return mixed, gtok, ggate.T, gup.T, gdown


def solution(mesh):
    in_specs = (
        P(("gy", "gx"), "gz"),
        P(("gz", "gy"), "gx"),
        P(("gz", "gy"), "gx"),
        P(("gx", "gy"), "gz"),
        P(("gy", "gx"), "gz"),
    )
    out_specs = (
        P(("gy", "gx"), "gz"),
        P(("gy", "gx"), "gz"),
        P(("gz", "gy"), "gx"),
        P(("gz", "gy"), "gx"),
        P(("gx", "gy"), "gz"),
    )
    return jax.shard_map(body, mesh=mesh, in_specs=in_specs, out_specs=out_specs, check_vma=False)
```

```python
import functools
import math

import jax
import jax.numpy as jnp
from jax import lax
from jax.experimental import pallas as pl
from jax.experimental.pallas import tpu as pltpu
from jax.sharding import PartitionSpec as P

BF = jnp.bfloat16
F32 = jnp.float32
ORDER = "H1 P1 R0 H3 P3 D0 H2 P2 R1 R3 F0 D1 R2 D3 F1 G0 D2 F3 G1 F2 G3 G2"
MESH_ID = pl.DeviceIdType.MESH
LOW = 512
HIGH = 1024 - LOW
UNIT = 231


def dot_nn(a, b):
    return lax.dot_general(a, b, (((1,), (0,)), ((), ())), preferred_element_type=F32)


def dot_nt(a, b):
    return lax.dot_general(a, b, (((1,), (1,)), ((), ())), preferred_element_type=F32)


LAYOUT = {}
COUNT = 0
for name, size in (
    ("zh", 2), ("y", 6), ("x", 6), ("x1", 6), ("y2", 6), ("wx", 4), ("wc", 4), ("wd", 1),
    ("rh", 16), ("rp", 16), ("lh", 4), ("lp", 4), ("ag", 16), ("af", 4),
    ("ox", 8), ("oy", 8), ("oz", 2), ("py", 32), ("px", 8), ("gc", 4), ("gx", 4), ("gd", 1),
):
    LAYOUT[name] = COUNT
    COUNT += size


def kernel(
    factor,
    tok_ref, cot_ref, gw_ref, uw_ref, wd_ref,
    mixed_ref, gtok_ref, ggate_ref, gup_ref, gdown_ref,
    acts, w_loc, w, wd, parts, zs_h, zr_h, rl_h, zs_p, zr_p, rl_p, mids, mids_t, gw_in, uw_in, tok_in, cot_in, wd_in, wd_own,
    o_send, o_recv, o_own, p_own, p_recv, p_sum, px_recv, y_own, y_recv, z_send, z_recv,
    gc_send, gc_recv, g_acc, g_out, gx_send, gx_recv, gd_send, gd_recv, gd_own,
    send, recv, local,
):
    gx, gy, z = lax.axis_index("gx"), lax.axis_index("gy"), lax.axis_index("gz")
    y, h = gx // 2, gx % 2
    x, c = gy // 2, gy % 2
    oc = 1 - c

    def at(dx=0, dc=0, dy=0, dh=0, dz=0):
        px, py, pz = (x + dx) % 4, (y + dy) % 4, (z + dz) % 4
        ph, pc = (h + dh) % 2, (c + dc) % 2
        return (py * 2 + ph, px * 2 + pc, pz)

    def copy(src, dst, who, name, s_off, r_off=None):
        r_off = s_off if r_off is None else r_off
        return pltpu.make_async_remote_copy(
            src_ref=src, dst_ref=dst,
            send_sem=send.at[LAYOUT[name] + s_off], recv_sem=recv.at[LAYOUT[name] + r_off],
            device_id=who, device_id_type=MESH_ID,
        )

    started = []
    pending = []

    def go(*args):
        cp = copy(*args)
        cp.start()
        started.append(cp)
        return cp

    def go_if(cond, *args):
        @pl.when(cond)
        def _():
            copy(*args).start()

        pending.append((cond, args))

    def wait_if(cond, *args):
        @pl.when(cond)
        def _():
            copy(*args).wait_recv()

    inner = (z == 1) | (z == 2)
    via = 1 + z // 3
    far = 3 - z
    relay_to = 3 * ((2 - z + 4) % 4 % 2)

    peers = (
        [at(dx=k) for k in (1, 2, 3)] + [at(dy=k) for k in (1, 2, 3)]
        + [at(dz=k) for k in (1, 2, 3)] + [at(dh=1), at(dc=1)]
    )
    loads = [
        pltpu.make_async_copy(src, dst, local.at[i])
        for i, (src, dst) in enumerate(((uw_ref, uw_in), (gw_ref, gw_in), (cot_ref, cot_in), (tok_ref, tok_in), (wd_ref, wd_in)))
    ]
    for load in loads:
        load.start()
    barrier = pltpu.get_barrier_semaphore()
    for who in peers:
        pl.semaphore_signal(barrier, inc=1, device_id=who, device_id_type=MESH_ID)
    zeros = jnp.zeros((128, 256), BF)
    for n, ref in ((0, uw_in), (1, gw_in)):
        loads[n].wait()
        flat = ref[...].T
        for j in range(8):
            base = n * 512 + (j % 2) * 256
            w_loc[j // 2, :, base:base + 256] = zeros
            w_loc[j // 2, :, base:base + UNIT] = flat[:, UNIT * j:UNIT * (j + 1)]
    row_own = pl.multiple_of((x * 2 + c) * 128, 128)
    w_rows = pl.ds(row_own, 128)
    w[w_rows, :] = w_loc[x]
    for load in loads[2:]:
        load.wait()
    acts[0, 0, 0, 0:16, :] = cot_in[...]
    acts[1, 0, 0, 0:16, :] = tok_in[...]
    wd_rows = pl.ds(pl.multiple_of(c * 256, 256), 256)
    wd_own[224:256, :] = jnp.zeros((32, 1024), BF)
    wd_own[0:UNIT, :] = wd_in[...]
    wd[wd_rows, :] = wd_own[...]
    pl.semaphore_wait(barrier, len(peers))

    zh = [
        go((cot_in, tok_in)[i], acts.at[i, 0, 0, pl.ds(16, 16), :], at(dh=1), "zh", i) for i in (0, 1)
    ]
    wdc = go(wd_own, wd.at[wd_rows, :], at(dc=1), "wd", 0)
    wx = {}
    for r in (1, 3, 2):
        wx[r] = go(w_loc.at[(x + r) % 4], w.at[w_rows, :], at(dx=r), "wx", r)
    wc = [go(w_loc.at[x], w.at[w_rows, :], at(dc=1), "wc", 0)]

    @pl.when(jnp.logical_not(inner))
    def _():
        zr_h[:, far] = jnp.zeros((4, 32, 512), BF)
        zr_p[:, far] = jnp.zeros((4, 32, 1024), BF)

    low, high = pl.ds(0, LOW), pl.ds(LOW, HIGH)

    def spread_own(i):
        zh[i].wait_recv()
        src = acts.at[i, 0, 0]
        over_y = [go(src, acts.at[i, 0, m], at(dy=m), "y", i * 3 + m - 1) for m in (1, 3, 2)]
        over_x = [
            go(src.at[:, high], acts.at[i, k, 0, :, high], at(dx=k), "x1", i * 3 + k - 1)
            for k in (1, 3, 2)
        ]
        return over_y, over_x

    def spread_x(i, ks):
        for k in ks:
            src, dst = acts.at[i, 0, :, :, low], acts.at[i, k, :, :, low]
            slots[i, k] = go(src, dst, at(dx=k), "x", i * 3 + k - 1)

    def spread_y(i, copies):
        for cp in copies:
            cp.wait_recv()
        out = []
        for m in (1, 3, 2):
            src, dst = acts.at[i, pl.ds(1, 3), 0, :, high], acts.at[i, pl.ds(1, 3), m, :, high]
            out.append(go(src, dst, at(dy=m), "y2", i * 3 + m - 1))
        rights[i] = out

    def slot_ready(i, k):
        for cp in rights[i]:
            cp.wait_recv()
        rights[i] = []
        slots[i, k].wait_recv()

    slots, rights = {}, {}

    def scatter(k, src, dst, relay, name, relay_name):
        for m in range(4):
            rows = src.at[k, pl.ds(32 * m, 32)]
            direct = (z == 1) if m == 0 else (z == 2) if m == 3 else (z != m)
            go_if(direct, rows, dst.at[k, z], (gx, gy, m), name, k * 4 + m, k * 4 + z)
            if m in (0, 3):
                go_if(z == 3 - m, rows, relay.at[k], (gx, gy, via), relay_name, k)

    def hidden_grad(k):
        def tile(j, carry):
            rows = pl.ds(pl.multiple_of(j * 256, 256), 256)
            part = dot_nt(acts[0, k].reshape(128, 1024), wd[rows, :])
            zs_h[k, :, rows] = part.astype(BF)
            parts[k, :, pl.ds(pl.multiple_of(j * 256 + 1024, 256), 256)] = part
            return carry

        lax.fori_loop(0, 2, tile, 0, unroll=True)
        scatter(k, zs_h, zr_h, rl_h, "rh", "lh")

    def gate_up(k):
        def tile(j, carry):
            cols = pl.ds(pl.multiple_of(j * 256, 256), 256)
            part = dot_nn(acts[1, k].reshape(128, 1024), w[:, cols])
            zs_p[k, :, cols] = part.astype(BF)
            parts[k, :, cols] = part
            return carry

        lax.fori_loop(0, 4, tile, 0, unroll=True)
        scatter(k, zs_p, zr_p, rl_p, "rp", "lp")

    def relay(k):
        rows = pl.ds(pl.multiple_of(relay_to * 32, 32), 32)

        @pl.when(inner)
        def _():
            copy(rl_h.at[k], rl_h.at[k], (gx, gy, 3 - relay_to), "lh", k).wait_recv()
            zs_h[k, rows, :] = (parts[k, rows, 1024:1536] + rl_h[k].astype(F32)).astype(BF)
            copy(rl_p.at[k], rl_p.at[k], (gx, gy, 3 - relay_to), "lp", k).wait_recv()
            zs_p[k, rows, :] = (parts[k, rows, 0:1024] + rl_p[k].astype(F32)).astype(BF)

        for m in (0, 3):
            sel = z == (2 if m == 0 else 1)
            piece = pl.ds(32 * m, 32)
            go_if(sel, zs_h.at[k, piece], zr_h.at[k, z], (gx, gy, m), "rh", k * 4 + m, k * 4 + z)
            go_if(sel, zs_p.at[k, piece], zr_p.at[k, z], (gx, gy, m), "rp", k * 4 + m, k * 4 + z)

    def mix(k):
        for s in range(4):
            cond = (z != s) & (z != 3 - s) if s in (0, 3) else z != s
            wait_if(cond, zs_h.at[k, pl.ds(0, 32)], zr_h.at[k, s], (gx, gy, s), "rh", k * 4 + s)
            wait_if(cond, zs_p.at[k, pl.ds(0, 32)], zr_p.at[k, s], (gx, gy, s), "rp", k * 4 + s)
        mine = pl.ds(pl.multiple_of(z * 32, 32), 32)
        out = pl.ds(pl.multiple_of(z * 32 + 128 * k, 32), 32)

        def tile(j, carry):
            def total(got, off, skip):
                here = pl.ds(pl.multiple_of(j * 128 + off, 128), 128)
                mid = pl.ds(pl.multiple_of(j * 128 + off + skip, 128), 128)
                return (
                    (parts[k, mine, mid] + got[k, (z + 1) % 4, :, here].astype(F32))
                    + (got[k, (z + 2) % 4, :, here].astype(F32) + got[k, (z + 3) % 4, :, here].astype(F32))
                )

            up = total(zr_p, 0, 0)
            gate = total(zr_p, 512, 0)
            grad = total(zr_h, 0, 1024)
            sigma = jax.nn.sigmoid(gate)
            swish = gate * sigma

            def put(n, value):
                mids[out, pl.ds(pl.multiple_of(j * 128 + 512 * n, 128), 128)] = value.astype(BF)

            put(0, grad * swish)
            put(1, grad * up * sigma * (1.0 + gate * (1.0 - sigma)))
            put(2, swish * up)
            return carry

        lax.fori_loop(0, 4, tile, 0, unroll=True)
        block = mids.at[out, :]
        for m in range(4):
            cond = (z != m) & (z != 3 - m) if m in (0, 3) else z != m
            go_if(cond, block, block, (gx, gy, m), "ag", k * 4 + m, k * 4 + z)

    def forward(k):
        for m in (0, 3):
            sel = z == (1 if m == 0 else 2)
            block = mids.at[pl.ds(128 * k + 32 * (3 - m), 32), :]
            wait_if(sel, block, block, (gx, gy, 3 - m), "ag", k * 4 + 3 - m)
            go_if(sel, block, block, (gx, gy, m), "af", k, k * 4 - LAYOUT["af"] + LAYOUT["ag"] + 3 - m)

    def arrived(k):
        for s in range(4):
            cond = z != s
            if s == 0:
                cond = cond & (z != 2)
            if s == 3:
                cond = cond & (z != 1)
            block = mids.at[pl.ds(128 * k + 32 * s, 32), :]
            wait_if(cond, block, block, (gx, gy, s), "ag", k * 4 + s)

    def out_block(n, k):
        slot = pl.ds(128 * k, 128)

        def tile(j):
            cols = slice(256 * j, 256 * (j + 1))
            if n == 0:
                part = dot_nt(mids[slot, 0:1024], w[cols, :])
            else:
                part = dot_nn(mids[slot, 1024:1536], wd[:, cols])
            if k or 256 * j >= LOW:
                o_send[n, k, :, cols] = part.astype(BF)
            if k == 0:
                o_own[n, :, cols] = part
            elif 256 * j >= LOW:
                p_own[n, k, :, 256 * j - LOW:256 * (j + 1) - LOW] = part[0:32]

        for j in range(4):
            tile(j)
        if k:
            go(o_send.at[n, k, :, low], o_recv.at[n, k], at(dx=4 - k), "ox", n * 4 + k)
        for m in (1, 3, 2):
            src = o_send.at[n, k, pl.ds(32 * m, 32), high]
            go(src, p_recv.at[n, k, m], at(dy=4 - m), "py", n * 16 + k * 4 + m)

    def slot_cols(k):
        return slice(128 * k, 128 * (k + 1))

    def project(k):
        arrived(k)
        out_block(0, k)
        out_block(1, k)
        for j in range(12):
            mids_t[128 * j:128 * (j + 1), slot_cols(k)] = mids[slot_cols(k), 128 * j:128 * (j + 1)].T

    cot_y, cot_x = spread_own(0)
    tok_y, tok_x = spread_own(1)
    for cp in cot_y:
        cp.wait_recv()
    spread_x(0, (1, 3))
    wdc.wait_recv()
    hidden_grad(0)
    for cp in tok_y:
        cp.wait_recv()
    spread_x(1, (1, 3))
    spread_y(0, cot_x)
    spread_y(1, tok_x)
    for r in (1, 3, 2):
        wx[r].wait_recv()
        rows = pl.ds(pl.multiple_of(((x - r + 4) % 4 * 2 + c) * 128, 128), 128)
        wc.append(go(w.at[rows, :], w.at[rows, :], at(dc=1), "wc", r))
    spread_x(0, (2,))
    spread_x(1, (2,))
    for cp in wc:
        cp.wait_recv()
    gate_up(0)

    def slot_h(k):
        slot_ready(0, k)
        hidden_grad(k)

    def slot_p(k):
        slot_ready(1, k)
        gate_up(k)

    steps = {"H": slot_h, "P": slot_p, "R": relay, "D": mix, "F": forward, "G": project}
    for step in ORDER.split():
        steps[step[0]](int(step[1]))

    early = list(started), list(pending)
    del started[:], pending[:]

    def drain(copies, conds):
        for cp in copies:
            cp.wait_send()
        for cond, args in conds:
            @pl.when(cond)
            def _():
                copy(*args).wait_send()

    def token_cols(to, side):
        cols = pl.ds(pl.multiple_of((to * 2 + side) * 128, 128), 128)
        return acts[1, :, :, :, cols].reshape(512, 128)

    gc = {}
    for r in (1, 3, 2, 0):
        to = (x + r) % 4
        both = jnp.concatenate([token_cols(to, oc), token_cols(to, c)], axis=1)
        for n in range(4):
            part = dot_nn(mids_t[256 * n:256 * (n + 1)], both) * factor
            gc_send[r, n] = part[0:240, 0:128].astype(BF)
            g_acc[r, n] = part[0:240, 128:256]
        gc[r] = go(gc_send.at[r], gc_recv.at[r], at(dc=1), "gc", r)
    for r in (1, 3, 2):
        gc[r].wait_recv()
        gx_send[r] = (g_acc[r] + gc_recv[r].astype(F32)).astype(BF)
        go(gx_send.at[r], gx_recv.at[x], at(dx=r), "gx", r)

    drain(*early)
    theirs = pl.ds(pl.multiple_of(oc * 256 + 1024, 256), 256)
    ours = pl.ds(pl.multiple_of(c * 256 + 1024, 256), 256)

    def down_theirs(j, carry):
        cols = pl.ds(pl.multiple_of(j * 256, 256), 256)
        gd_send[:, cols] = (dot_nn(mids_t[theirs, :], acts[0, :, :, :, cols].reshape(512, 256)) * factor).astype(BF)
        return carry

    lax.fori_loop(0, 4, down_theirs, 0, unroll=True)
    gd = go(gd_send, gd_recv, at(dc=1), "gd", 0)

    oy, px = {}, {}
    for n in (0, 1):
        for k in range(4):
            for m in (1, 2, 3):
                src = o_send.at[n, k, pl.ds(32 * m, 32), high]
                copy(src, p_recv.at[n, k, m], at(dy=4 - m), "py", n * 16 + k * 4 + m).wait_recv()
            mine = p_own[n, k] if k else o_own[n, 0:32, LOW:1024]
            p_sum[n, k] = (mine + p_recv[n, k, 1].astype(F32)) + (
                p_recv[n, k, 2].astype(F32) + p_recv[n, k, 3].astype(F32)
            )
            if k:
                px[n, k] = go(p_sum.at[n, k], px_recv.at[n, k], at(dx=4 - k), "px", n * 4 + k)
        for k in (1, 2, 3):
            src = o_send.at[n, k, :, low]
            copy(src, o_recv.at[n, k], at(dx=4 - k), "ox", n * 4 + k).wait_recv()
        y_own[n] = (o_own[n, :, 0:LOW] + o_recv[n, 1].astype(F32)) + (
            o_recv[n, 2].astype(F32) + o_recv[n, 3].astype(F32)
        )
        for m in (1, 3, 2):
            oy[n, m] = go(
                y_own.at[n, pl.ds(32 * m, 32), :], y_recv.at[n, m], at(dy=4 - m), "oy", n * 4 + m
            )

    def down_ours(j, carry):
        cols = pl.ds(pl.multiple_of(j * 256, 256), 256)
        gd_own[:, cols] = dot_nn(mids_t[ours, :], acts[0, :, :, :, cols].reshape(512, 256)) * factor
        return carry

    lax.fori_loop(0, 4, down_ours, 0, unroll=True)
    gd.wait_recv()
    gdown_ref[...] = gd_own[0:UNIT, :] + gd_recv[0:UNIT, :].astype(F32)

    oz = []
    for n in (0, 1):
        for m in (1, 2, 3):
            oy[n, m].wait_recv()
        z_send[n, :, 0:LOW] = (y_own[n, 0:32, :] + y_recv[n, 1]) + (y_recv[n, 2] + y_recv[n, 3])
        for k in (1, 2, 3):
            px[n, k].wait_recv()
        z_send[n, :, LOW:1024] = (p_sum[n, 0] + px_recv[n, 1]) + (px_recv[n, 2] + px_recv[n, 3])
        oz.append(go(z_send.at[n, pl.ds(16, 16), :], z_recv.at[n], at(dh=1), "oz", n))

    gc[0].wait_recv()
    for r in (1, 2, 3):
        slot = (x - r + 4) % 4
        copy(gx_send.at[r], gx_recv.at[slot], at(dx=r), "gx", r).wait_recv()
    for p in range(4):
        @pl.when(x == p)
        def _():
            g_out[...] = g_acc[0] + gc_recv[0].astype(F32)

        @pl.when(x != p)
        def _():
            g_out[...] = gx_recv[p].astype(F32)

        for n, out in ((0, gup_ref), (1, ggate_ref)):
            for j in (0, 1):
                row = UNIT * (2 * p + j)
                out[row:row + UNIT, :] = g_out[2 * n + j, 0:UNIT, :]

    for n, out in ((0, gtok_ref), (1, mixed_ref)):
        oz[n].wait_recv()
        out[...] = (z_send[n, 0:16, :] + z_recv[n]).astype(BF)

    drain(started, pending)


def write_out(*refs):
    sems = refs[10]
    copies = [pltpu.make_async_copy(refs[i], refs[5 + i], sems.at[i]) for i in range(5)]
    for cp in copies:
        cp.start()
    for cp in copies:
        cp.wait()


def body(tokens, gate_weight, up_weight, down_weight, cotangent):
    vmem = pl.BlockSpec(memory_space=pltpu.VMEM)
    factor = 1.0 / math.sqrt(1024)
    anywhere = pl.BlockSpec(memory_space=pl.ANY)
    results = pl.pallas_call(
        functools.partial(kernel, factor),
        name="swiglu",
        out_shape=(
            jax.ShapeDtypeStruct((16, 1024), BF),
            jax.ShapeDtypeStruct((16, 1024), BF),
            jax.ShapeDtypeStruct((1848, 128), F32),
            jax.ShapeDtypeStruct((1848, 128), F32),
            jax.ShapeDtypeStruct((UNIT, 1024), F32),
        ),
        in_specs=[anywhere] * 5,
        out_specs=[vmem] * 5,
        scratch_shapes=[
            pltpu.VMEM((2, 4, 4, 32, 1024), BF),
            pltpu.VMEM((4, 128, 1024), BF),
            pltpu.VMEM((1024, 1024), BF),
            pltpu.VMEM((512, 1024), BF),
            pltpu.VMEM((4, 128, 1536), F32),
            pltpu.VMEM((4, 128, 512), BF),
            pltpu.VMEM((4, 4, 32, 512), BF),
            pltpu.VMEM((4, 32, 512), BF),
            pltpu.VMEM((4, 128, 1024), BF),
            pltpu.VMEM((4, 4, 32, 1024), BF),
            pltpu.VMEM((4, 32, 1024), BF),
            pltpu.VMEM((512, 1536), BF),
            pltpu.VMEM((1536, 512), BF),
            pltpu.VMEM((1848, 128), BF),
            pltpu.VMEM((1848, 128), BF),
            pltpu.VMEM((16, 1024), BF),
            pltpu.VMEM((16, 1024), BF),
            pltpu.VMEM((UNIT, 1024), BF),
            pltpu.VMEM((256, 1024), BF),
            pltpu.VMEM((2, 4, 128, 1024), BF),
            pltpu.VMEM((2, 4, 128, LOW), BF),
            pltpu.VMEM((2, 128, 1024), F32),
            pltpu.VMEM((2, 4, 32, HIGH), F32),
            pltpu.VMEM((2, 4, 4, 32, HIGH), BF),
            pltpu.VMEM((2, 4, 32, HIGH), F32),
            pltpu.VMEM((2, 4, 32, HIGH), F32),
            pltpu.VMEM((2, 128, LOW), F32),
            pltpu.VMEM((2, 4, 32, LOW), F32),
            pltpu.VMEM((2, 32, 1024), F32),
            pltpu.VMEM((2, 16, 1024), F32),
            pltpu.VMEM((4, 4, 240, 128), BF),
            pltpu.VMEM((4, 4, 240, 128), BF),
            pltpu.VMEM((4, 4, 240, 128), F32),
            pltpu.VMEM((4, 240, 128), F32),
            pltpu.VMEM((4, 4, 240, 128), BF),
            pltpu.VMEM((4, 4, 240, 128), BF),
            pltpu.VMEM((256, 1024), BF),
            pltpu.VMEM((256, 1024), BF),
            pltpu.VMEM((256, 1024), F32),
            pltpu.SemaphoreType.DMA((COUNT,)),
            pltpu.SemaphoreType.DMA((COUNT,)),
            pltpu.SemaphoreType.DMA((5,)),
        ],
        compiler_params=pltpu.CompilerParams(
            collective_id=1, has_side_effects=True, vmem_limit_bytes=48 << 20
        ),
    )(tokens, cotangent, gate_weight.T, up_weight.T, down_weight)
    mixed, gtok, ggate, gup, gdown = pl.pallas_call(
        write_out,
        name="write_out",
        out_shape=tuple(jax.ShapeDtypeStruct(a.shape, a.dtype) for a in results),
        in_specs=[vmem] * 5,
        out_specs=[anywhere] * 5,
        scratch_shapes=[pltpu.SemaphoreType.DMA((5,))],
        compiler_params=pltpu.CompilerParams(vmem_limit_bytes=16 << 20),
    )(*results)
    return mixed, gtok, ggate.T, gup.T, gdown


def solution(mesh):
    in_specs = (
        P(("gy", "gx"), "gz"),
        P(("gz", "gy"), "gx"),
        P(("gz", "gy"), "gx"),
        P(("gx", "gy"), "gz"),
        P(("gy", "gx"), "gz"),
    )
    out_specs = (
        P(("gy", "gx"), "gz"),
        P(("gy", "gx"), "gz"),
        P(("gz", "gy"), "gx"),
        P(("gz", "gy"), "gx"),
        P(("gx", "gy"), "gz"),
    )
    return jax.shard_map(body, mesh=mesh, in_specs=in_specs, out_specs=out_specs, check_vma=False)
```

```python
import functools
import math

import jax
import jax.numpy as jnp
from jax import lax
from jax.experimental import pallas as pl
from jax.experimental.pallas import tpu as pltpu
from jax.sharding import PartitionSpec as P

BF = jnp.bfloat16
F32 = jnp.float32
ORDER = "H1 P1 R0 H3 P3 D0 H2 P2 R1 R3 F0 D1 R2 D3 F1 G0 D2 F3 G1 F2 G3 G2"
MESH_ID = pl.DeviceIdType.MESH
LOW = 512
HIGH = 1024 - LOW
UNIT = 231


def dot_nn(a, b):
    return lax.dot_general(a, b, (((1,), (0,)), ((), ())), preferred_element_type=F32)


def dot_nt(a, b):
    return lax.dot_general(a, b, (((1,), (1,)), ((), ())), preferred_element_type=F32)


LAYOUT = {}
COUNT = 0
for name, size in (
    ("zh", 2), ("y", 6), ("x", 6), ("x1", 6), ("y2", 6), ("wx", 4), ("wc", 4), ("wd", 1),
    ("rh", 16), ("rp", 16), ("lh", 4), ("lp", 4), ("ag", 16), ("af", 4),
    ("ox", 8), ("oy", 8), ("oz", 2), ("py", 32), ("px", 8), ("gc", 4), ("gx", 4), ("gd", 1),
):
    LAYOUT[name] = COUNT
    COUNT += size


def kernel(
    factor,
    tok_ref, cot_ref, gw_ref, uw_ref, wd_ref,
    mixed_ref, gtok_ref, ggate_ref, gup_ref, gdown_ref,
    acts, w_loc, w, wd, parts, zs_h, zr_h, rl_h, zs_p, zr_p, rl_p, mids, mids_t, tok_in, cot_in, wd_in, wd_own,
    o_send, o_recv, o_own, p_own, p_recv, p_sum, px_recv, y_own, y_recv, z_send, z_recv,
    gc_send, gc_recv, g_acc, g_out, gx_send, gx_recv, gd_send, gd_recv, gd_own,
    send, recv, local,
):
    gx, gy, z = lax.axis_index("gx"), lax.axis_index("gy"), lax.axis_index("gz")
    y, h = gx // 2, gx % 2
    x, c = gy // 2, gy % 2
    oc = 1 - c

    def at(dx=0, dc=0, dy=0, dh=0, dz=0):
        px, py, pz = (x + dx) % 4, (y + dy) % 4, (z + dz) % 4
        ph, pc = (h + dh) % 2, (c + dc) % 2
        return (py * 2 + ph, px * 2 + pc, pz)

    def copy(src, dst, who, name, s_off, r_off=None):
        r_off = s_off if r_off is None else r_off
        return pltpu.make_async_remote_copy(
            src_ref=src, dst_ref=dst,
            send_sem=send.at[LAYOUT[name] + s_off], recv_sem=recv.at[LAYOUT[name] + r_off],
            device_id=who, device_id_type=MESH_ID,
        )

    started = []
    pending = []

    def go(*args):
        cp = copy(*args)
        cp.start()
        started.append(cp)
        return cp

    def go_if(cond, *args):
        @pl.when(cond)
        def _():
            copy(*args).start()

        pending.append((cond, args))

    def wait_if(cond, *args):
        @pl.when(cond)
        def _():
            copy(*args).wait_recv()

    inner = (z == 1) | (z == 2)
    via = 1 + z // 3
    far = 3 - z
    relay_to = 3 * ((2 - z + 4) % 4 % 2)

    peers = (
        [at(dx=k) for k in (1, 2, 3)] + [at(dy=k) for k in (1, 2, 3)]
        + [at(dz=k) for k in (1, 2, 3)] + [at(dh=1), at(dc=1)]
    )
    loads = [
        pltpu.make_async_copy(src, dst, local.at[i])
        for i, (src, dst) in enumerate(((cot_ref, cot_in), (tok_ref, tok_in), (wd_ref, wd_in)))
    ]
    for load in loads:
        load.start()
    barrier = pltpu.get_barrier_semaphore()
    for who in peers:
        pl.semaphore_signal(barrier, inc=1, device_id=who, device_id_type=MESH_ID)
    zeros = jnp.zeros((128, 256), BF)
    for n, ref in ((0, uw_ref), (1, gw_ref)):
        for j in range(8):
            base = n * 512 + (j % 2) * 256
            w_loc[j // 2, :, base:base + 256] = zeros
            w_loc[j // 2, :, base:base + UNIT] = ref[:, UNIT * j:UNIT * (j + 1)]
    row_own = pl.multiple_of((x * 2 + c) * 128, 128)
    w_rows = pl.ds(row_own, 128)
    w[w_rows, :] = w_loc[x]
    for load in loads:
        load.wait()
    acts[0, 0, 0, 0:16, :] = cot_in[...]
    acts[1, 0, 0, 0:16, :] = tok_in[...]
    wd_rows = pl.ds(pl.multiple_of(c * 256, 256), 256)
    wd_own[224:256, :] = jnp.zeros((32, 1024), BF)
    wd_own[0:UNIT, :] = wd_in[...]
    wd[wd_rows, :] = wd_own[...]
    pl.semaphore_wait(barrier, len(peers))

    zh = [
        go((cot_in, tok_in)[i], acts.at[i, 0, 0, pl.ds(16, 16), :], at(dh=1), "zh", i) for i in (0, 1)
    ]
    wdc = go(wd_own, wd.at[wd_rows, :], at(dc=1), "wd", 0)
    wx = {}
    for r in (1, 3, 2):
        wx[r] = go(w_loc.at[(x + r) % 4], w.at[w_rows, :], at(dx=r), "wx", r)
    wc = [go(w_loc.at[x], w.at[w_rows, :], at(dc=1), "wc", 0)]

    @pl.when(jnp.logical_not(inner))
    def _():
        zr_h[:, far] = jnp.zeros((4, 32, 512), BF)
        zr_p[:, far] = jnp.zeros((4, 32, 1024), BF)

    low, high = pl.ds(0, LOW), pl.ds(LOW, HIGH)

    def spread_own(i):
        zh[i].wait_recv()
        src = acts.at[i, 0, 0]
        over_y = [go(src, acts.at[i, 0, m], at(dy=m), "y", i * 3 + m - 1) for m in (1, 3, 2)]
        over_x = [
            go(src.at[:, high], acts.at[i, k, 0, :, high], at(dx=k), "x1", i * 3 + k - 1)
            for k in (1, 3, 2)
        ]
        return over_y, over_x

    def spread_x(i, ks):
        for k in ks:
            src, dst = acts.at[i, 0, :, :, low], acts.at[i, k, :, :, low]
            slots[i, k] = go(src, dst, at(dx=k), "x", i * 3 + k - 1)

    def spread_y(i, copies):
        for cp in copies:
            cp.wait_recv()
        out = []
        for m in (1, 3, 2):
            src, dst = acts.at[i, pl.ds(1, 3), 0, :, high], acts.at[i, pl.ds(1, 3), m, :, high]
            out.append(go(src, dst, at(dy=m), "y2", i * 3 + m - 1))
        rights[i] = out

    def slot_ready(i, k):
        for cp in rights[i]:
            cp.wait_recv()
        rights[i] = []
        slots[i, k].wait_recv()

    slots, rights = {}, {}

    def scatter(k, src, dst, relay, name, relay_name):
        for m in range(4):
            rows = src.at[k, pl.ds(32 * m, 32)]
            direct = (z == 1) if m == 0 else (z == 2) if m == 3 else (z != m)
            go_if(direct, rows, dst.at[k, z], (gx, gy, m), name, k * 4 + m, k * 4 + z)
            if m in (0, 3):
                go_if(z == 3 - m, rows, relay.at[k], (gx, gy, via), relay_name, k)

    def hidden_grad(k):
        def tile(j, carry):
            rows = pl.ds(pl.multiple_of(j * 256, 256), 256)
            part = dot_nt(acts[0, k].reshape(128, 1024), wd[rows, :])
            zs_h[k, :, rows] = part.astype(BF)
            parts[k, :, pl.ds(pl.multiple_of(j * 256 + 1024, 256), 256)] = part
            return carry

        lax.fori_loop(0, 2, tile, 0, unroll=True)
        scatter(k, zs_h, zr_h, rl_h, "rh", "lh")

    def gate_up(k):
        def tile(j, carry):
            cols = pl.ds(pl.multiple_of(j * 256, 256), 256)
            part = dot_nn(acts[1, k].reshape(128, 1024), w[:, cols])
            zs_p[k, :, cols] = part.astype(BF)
            parts[k, :, cols] = part
            return carry

        lax.fori_loop(0, 4, tile, 0, unroll=True)
        scatter(k, zs_p, zr_p, rl_p, "rp", "lp")

    def relay(k):
        rows = pl.ds(pl.multiple_of(relay_to * 32, 32), 32)

        @pl.when(inner)
        def _():
            copy(rl_h.at[k], rl_h.at[k], (gx, gy, 3 - relay_to), "lh", k).wait_recv()
            zs_h[k, rows, :] = (parts[k, rows, 1024:1536] + rl_h[k].astype(F32)).astype(BF)
            copy(rl_p.at[k], rl_p.at[k], (gx, gy, 3 - relay_to), "lp", k).wait_recv()
            zs_p[k, rows, :] = (parts[k, rows, 0:1024] + rl_p[k].astype(F32)).astype(BF)

        for m in (0, 3):
            sel = z == (2 if m == 0 else 1)
            piece = pl.ds(32 * m, 32)
            go_if(sel, zs_h.at[k, piece], zr_h.at[k, z], (gx, gy, m), "rh", k * 4 + m, k * 4 + z)
            go_if(sel, zs_p.at[k, piece], zr_p.at[k, z], (gx, gy, m), "rp", k * 4 + m, k * 4 + z)

    def mix(k):
        for s in range(4):
            cond = (z != s) & (z != 3 - s) if s in (0, 3) else z != s
            wait_if(cond, zs_h.at[k, pl.ds(0, 32)], zr_h.at[k, s], (gx, gy, s), "rh", k * 4 + s)
            wait_if(cond, zs_p.at[k, pl.ds(0, 32)], zr_p.at[k, s], (gx, gy, s), "rp", k * 4 + s)
        mine = pl.ds(pl.multiple_of(z * 32, 32), 32)
        out = pl.ds(pl.multiple_of(z * 32 + 128 * k, 32), 32)

        def tile(j, carry):
            def total(got, off, skip):
                here = pl.ds(pl.multiple_of(j * 128 + off, 128), 128)
                mid = pl.ds(pl.multiple_of(j * 128 + off + skip, 128), 128)
                return (
                    (parts[k, mine, mid] + got[k, (z + 1) % 4, :, here].astype(F32))
                    + (got[k, (z + 2) % 4, :, here].astype(F32) + got[k, (z + 3) % 4, :, here].astype(F32))
                )

            up = total(zr_p, 0, 0)
            gate = total(zr_p, 512, 0)
            grad = total(zr_h, 0, 1024)
            sigma = jax.nn.sigmoid(gate)
            swish = gate * sigma

            def put(n, value):
                mids[out, pl.ds(pl.multiple_of(j * 128 + 512 * n, 128), 128)] = value.astype(BF)

            put(0, grad * swish)
            put(1, grad * up * sigma * (1.0 + gate * (1.0 - sigma)))
            put(2, swish * up)
            return carry

        lax.fori_loop(0, 4, tile, 0, unroll=True)
        block = mids.at[out, :]
        for m in range(4):
            cond = (z != m) & (z != 3 - m) if m in (0, 3) else z != m
            go_if(cond, block, block, (gx, gy, m), "ag", k * 4 + m, k * 4 + z)

    def forward(k):
        for m in (0, 3):
            sel = z == (1 if m == 0 else 2)
            block = mids.at[pl.ds(128 * k + 32 * (3 - m), 32), :]
            wait_if(sel, block, block, (gx, gy, 3 - m), "ag", k * 4 + 3 - m)
            go_if(sel, block, block, (gx, gy, m), "af", k, k * 4 - LAYOUT["af"] + LAYOUT["ag"] + 3 - m)

    def arrived(k):
        for s in range(4):
            cond = z != s
            if s == 0:
                cond = cond & (z != 2)
            if s == 3:
                cond = cond & (z != 1)
            block = mids.at[pl.ds(128 * k + 32 * s, 32), :]
            wait_if(cond, block, block, (gx, gy, s), "ag", k * 4 + s)

    def out_block(n, k):
        slot = pl.ds(128 * k, 128)

        def tile(j):
            cols = slice(256 * j, 256 * (j + 1))
            if n == 0:
                part = dot_nt(mids[slot, 0:1024], w[cols, :])
            else:
                part = dot_nn(mids[slot, 1024:1536], wd[:, cols])
            if k or 256 * j >= LOW:
                o_send[n, k, :, cols] = part.astype(BF)
            if k == 0:
                o_own[n, :, cols] = part
            elif 256 * j >= LOW:
                p_own[n, k, :, 256 * j - LOW:256 * (j + 1) - LOW] = part[0:32]

        for j in range(4):
            tile(j)
        if k:
            go(o_send.at[n, k, :, low], o_recv.at[n, k], at(dx=4 - k), "ox", n * 4 + k)
        for m in (1, 3, 2):
            src = o_send.at[n, k, pl.ds(32 * m, 32), high]
            go(src, p_recv.at[n, k, m], at(dy=4 - m), "py", n * 16 + k * 4 + m)

    def slot_cols(k):
        return slice(128 * k, 128 * (k + 1))

    def project(k):
        arrived(k)
        out_block(0, k)
        out_block(1, k)
        for j in range(12):
            mids_t[128 * j:128 * (j + 1), slot_cols(k)] = mids[slot_cols(k), 128 * j:128 * (j + 1)].T

    cot_y, cot_x = spread_own(0)
    tok_y, tok_x = spread_own(1)
    for cp in cot_y:
        cp.wait_recv()
    spread_x(0, (1, 3))
    wdc.wait_recv()
    hidden_grad(0)
    for cp in tok_y:
        cp.wait_recv()
    spread_x(1, (1, 3))
    spread_y(0, cot_x)
    spread_y(1, tok_x)
    for r in (1, 3, 2):
        wx[r].wait_recv()
        rows = pl.ds(pl.multiple_of(((x - r + 4) % 4 * 2 + c) * 128, 128), 128)
        wc.append(go(w.at[rows, :], w.at[rows, :], at(dc=1), "wc", r))
    spread_x(0, (2,))
    spread_x(1, (2,))
    for cp in wc:
        cp.wait_recv()
    gate_up(0)

    def slot_h(k):
        slot_ready(0, k)
        hidden_grad(k)

    def slot_p(k):
        slot_ready(1, k)
        gate_up(k)

    steps = {"H": slot_h, "P": slot_p, "R": relay, "D": mix, "F": forward, "G": project}
    for step in ORDER.split():
        steps[step[0]](int(step[1]))

    early = list(started), list(pending)
    del started[:], pending[:]

    def drain(copies, conds):
        for cp in copies:
            cp.wait_send()
        for cond, args in conds:
            @pl.when(cond)
            def _():
                copy(*args).wait_send()

    def token_cols(to, side):
        cols = pl.ds(pl.multiple_of((to * 2 + side) * 128, 128), 128)
        return acts[1, :, :, :, cols].reshape(512, 128)

    gc = {}
    for r in (1, 3, 2, 0):
        to = (x + r) % 4
        both = jnp.concatenate([token_cols(to, oc), token_cols(to, c)], axis=1)
        for n in range(4):
            part = dot_nn(mids_t[256 * n:256 * (n + 1)], both) * factor
            gc_send[r, n] = part[0:240, 0:128].astype(BF)
            g_acc[r, n] = part[0:240, 128:256]
        gc[r] = go(gc_send.at[r], gc_recv.at[r], at(dc=1), "gc", r)
    for r in (1, 3, 2):
        gc[r].wait_recv()
        gx_send[r] = (g_acc[r] + gc_recv[r].astype(F32)).astype(BF)
        go(gx_send.at[r], gx_recv.at[x], at(dx=r), "gx", r)

    drain(*early)
    theirs = pl.ds(pl.multiple_of(oc * 256 + 1024, 256), 256)
    ours = pl.ds(pl.multiple_of(c * 256 + 1024, 256), 256)

    def down_theirs(j, carry):
        cols = pl.ds(pl.multiple_of(j * 256, 256), 256)
        gd_send[:, cols] = (dot_nn(mids_t[theirs, :], acts[0, :, :, :, cols].reshape(512, 256)) * factor).astype(BF)
        return carry

    lax.fori_loop(0, 4, down_theirs, 0, unroll=True)
    gd = go(gd_send, gd_recv, at(dc=1), "gd", 0)

    oy, px = {}, {}
    for n in (0, 1):
        for k in range(4):
            for m in (1, 2, 3):
                src = o_send.at[n, k, pl.ds(32 * m, 32), high]
                copy(src, p_recv.at[n, k, m], at(dy=4 - m), "py", n * 16 + k * 4 + m).wait_recv()
            mine = p_own[n, k] if k else o_own[n, 0:32, LOW:1024]
            p_sum[n, k] = (mine + p_recv[n, k, 1].astype(F32)) + (
                p_recv[n, k, 2].astype(F32) + p_recv[n, k, 3].astype(F32)
            )
            if k:
                px[n, k] = go(p_sum.at[n, k], px_recv.at[n, k], at(dx=4 - k), "px", n * 4 + k)
        for k in (1, 2, 3):
            src = o_send.at[n, k, :, low]
            copy(src, o_recv.at[n, k], at(dx=4 - k), "ox", n * 4 + k).wait_recv()
        y_own[n] = (o_own[n, :, 0:LOW] + o_recv[n, 1].astype(F32)) + (
            o_recv[n, 2].astype(F32) + o_recv[n, 3].astype(F32)
        )
        for m in (1, 3, 2):
            oy[n, m] = go(
                y_own.at[n, pl.ds(32 * m, 32), :], y_recv.at[n, m], at(dy=4 - m), "oy", n * 4 + m
            )

    def down_ours(j, carry):
        cols = pl.ds(pl.multiple_of(j * 256, 256), 256)
        gd_own[:, cols] = dot_nn(mids_t[ours, :], acts[0, :, :, :, cols].reshape(512, 256)) * factor
        return carry

    lax.fori_loop(0, 4, down_ours, 0, unroll=True)
    gd.wait_recv()
    gdown_ref[...] = gd_own[0:UNIT, :] + gd_recv[0:UNIT, :].astype(F32)

    oz = []
    for n in (0, 1):
        for m in (1, 2, 3):
            oy[n, m].wait_recv()
        z_send[n, :, 0:LOW] = (y_own[n, 0:32, :] + y_recv[n, 1]) + (y_recv[n, 2] + y_recv[n, 3])
        for k in (1, 2, 3):
            px[n, k].wait_recv()
        z_send[n, :, LOW:1024] = (p_sum[n, 0] + px_recv[n, 1]) + (px_recv[n, 2] + px_recv[n, 3])
        oz.append(go(z_send.at[n, pl.ds(16, 16), :], z_recv.at[n], at(dh=1), "oz", n))

    gc[0].wait_recv()
    for r in (1, 2, 3):
        slot = (x - r + 4) % 4
        copy(gx_send.at[r], gx_recv.at[slot], at(dx=r), "gx", r).wait_recv()
    for p in range(4):
        @pl.when(x == p)
        def _():
            g_out[...] = g_acc[0] + gc_recv[0].astype(F32)

        @pl.when(x != p)
        def _():
            g_out[...] = gx_recv[p].astype(F32)

        for n, out in ((0, gup_ref), (1, ggate_ref)):
            for j in (0, 1):
                row = UNIT * (2 * p + j)
                out[row:row + UNIT, :] = g_out[2 * n + j, 0:UNIT, :]

    for n, out in ((0, gtok_ref), (1, mixed_ref)):
        oz[n].wait_recv()
        out[...] = (z_send[n, 0:16, :] + z_recv[n]).astype(BF)

    drain(started, pending)


def write_out(*refs):
    sems = refs[10]
    copies = [pltpu.make_async_copy(refs[i], refs[5 + i], sems.at[i]) for i in range(5)]
    for cp in copies:
        cp.start()
    for cp in copies:
        cp.wait()


def body(tokens, gate_weight, up_weight, down_weight, cotangent):
    vmem = pl.BlockSpec(memory_space=pltpu.VMEM)
    factor = 1.0 / math.sqrt(1024)
    anywhere = pl.BlockSpec(memory_space=pl.ANY)
    results = pl.pallas_call(
        functools.partial(kernel, factor),
        name="swiglu",
        out_shape=(
            jax.ShapeDtypeStruct((16, 1024), BF),
            jax.ShapeDtypeStruct((16, 1024), BF),
            jax.ShapeDtypeStruct((1848, 128), F32),
            jax.ShapeDtypeStruct((1848, 128), F32),
            jax.ShapeDtypeStruct((UNIT, 1024), F32),
        ),
        in_specs=[anywhere, anywhere, vmem, vmem, anywhere],
        out_specs=[vmem] * 5,
        scratch_shapes=[
            pltpu.VMEM((2, 4, 4, 32, 1024), BF),
            pltpu.VMEM((4, 128, 1024), BF),
            pltpu.VMEM((1024, 1024), BF),
            pltpu.VMEM((512, 1024), BF),
            pltpu.VMEM((4, 128, 1536), F32),
            pltpu.VMEM((4, 128, 512), BF),
            pltpu.VMEM((4, 4, 32, 512), BF),
            pltpu.VMEM((4, 32, 512), BF),
            pltpu.VMEM((4, 128, 1024), BF),
            pltpu.VMEM((4, 4, 32, 1024), BF),
            pltpu.VMEM((4, 32, 1024), BF),
            pltpu.VMEM((512, 1536), BF),
            pltpu.VMEM((1536, 512), BF),
            pltpu.VMEM((16, 1024), BF),
            pltpu.VMEM((16, 1024), BF),
            pltpu.VMEM((UNIT, 1024), BF),
            pltpu.VMEM((256, 1024), BF),
            pltpu.VMEM((2, 4, 128, 1024), BF),
            pltpu.VMEM((2, 4, 128, LOW), BF),
            pltpu.VMEM((2, 128, 1024), F32),
            pltpu.VMEM((2, 4, 32, HIGH), F32),
            pltpu.VMEM((2, 4, 4, 32, HIGH), BF),
            pltpu.VMEM((2, 4, 32, HIGH), F32),
            pltpu.VMEM((2, 4, 32, HIGH), F32),
            pltpu.VMEM((2, 128, LOW), F32),
            pltpu.VMEM((2, 4, 32, LOW), F32),
            pltpu.VMEM((2, 32, 1024), F32),
            pltpu.VMEM((2, 16, 1024), F32),
            pltpu.VMEM((4, 4, 240, 128), BF),
            pltpu.VMEM((4, 4, 240, 128), BF),
            pltpu.VMEM((4, 4, 240, 128), F32),
            pltpu.VMEM((4, 240, 128), F32),
            pltpu.VMEM((4, 4, 240, 128), BF),
            pltpu.VMEM((4, 4, 240, 128), BF),
            pltpu.VMEM((256, 1024), BF),
            pltpu.VMEM((256, 1024), BF),
            pltpu.VMEM((256, 1024), F32),
            pltpu.SemaphoreType.DMA((COUNT,)),
            pltpu.SemaphoreType.DMA((COUNT,)),
            pltpu.SemaphoreType.DMA((3,)),
        ],
        compiler_params=pltpu.CompilerParams(
            collective_id=1, has_side_effects=True, vmem_limit_bytes=48 << 20
        ),
    )(tokens, cotangent, gate_weight, up_weight, down_weight)
    mixed, gtok, ggate, gup, gdown = pl.pallas_call(
        write_out,
        name="write_out",
        out_shape=tuple(jax.ShapeDtypeStruct(a.shape, a.dtype) for a in results),
        in_specs=[vmem] * 5,
        out_specs=[anywhere] * 5,
        scratch_shapes=[pltpu.SemaphoreType.DMA((5,))],
        compiler_params=pltpu.CompilerParams(vmem_limit_bytes=16 << 20),
    )(*results)
    return mixed, gtok, ggate.T, gup.T, gdown


def solution(mesh):
    in_specs = (
        P(("gy", "gx"), "gz"),
        P(("gz", "gy"), "gx"),
        P(("gz", "gy"), "gx"),
        P(("gx", "gy"), "gz"),
        P(("gy", "gx"), "gz"),
    )
    out_specs = (
        P(("gy", "gx"), "gz"),
        P(("gy", "gx"), "gz"),
        P(("gz", "gy"), "gx"),
        P(("gz", "gy"), "gx"),
        P(("gx", "gy"), "gz"),
    )
    return jax.shard_map(body, mesh=mesh, in_specs=in_specs, out_specs=out_specs, check_vma=False)
```
